32 devices in a mesh: pairs: 8 (over z, y), tensor: 4 (over x, core).
Axes of the slice: x: 2, y: 2, z: 4, core: 2. Of those that a mesh axis runs over, the one named last changes fastest.
Arguments:
- queries: bfloat16 [2048, 4096], P('pairs', 'tensor'), may hold values from -100 to 100
- key_rows: bfloat16 [2048, 4096], P('pairs', 'tensor'), may hold values from -3.5 to 3.5
- value_rows: bfloat16 [2048, 4096], P('pairs', 'tensor'), may hold values from -12 to 12
- pair_ids: int32 [2048], P('pairs'), may hold values from 0 to 8, as said below
- out_weight: bfloat16 [4096, 4096], P('tensor', 'pairs'), may hold values from -0.09375 to 0.09375
- residual: bfloat16 [1536, 4096], P('pairs', 'tensor'), may hold values from -6 to 6
Outputs:
- hidden_out: bfloat16 [1536, 4096], P('pairs', 'tensor')
The draws below stay inside these ranges and needn't reach their ends.
Inputs may be any that keep to these rules, and one draw needn't show every extreme that they name: `pair_ids`: within each block of 256 rows the entries never fall; rows with a value below 8 come first and rows with value 8 form the block's tail; equal values below 8 form one pair. The used rows of blocks 2k and 2k + 1 together number at most 384, reached by some two blocks, and some block has no unused row.
All inputs are finite; a program needn't handle non-finite values.
Results may differ from the reference program's by a relative error of at most 0.0055.
Values may be sent and summed in bfloat16 or wider, within the bound.
A program may use at most 64 MiB of HBM per device.

```python
import jax
import jax.numpy as jnp
from jax import lax

D = 4096
HEADS = 64
HEAD = 64
CAP = 256
SLOTS = 8
ROWS = 192
PADROWS = 2048
TOKENS = 1536
N_PAIRS = 8
N_TENSOR = 4


def paired_rows(key):
    full_width = HEADS * HEAD
    base_query = jnp.clip(jax.random.normal(jax.random.fold_in(key, 11), (PADROWS, full_width), jnp.float32), -8.0, 8.0) * 0.35
    base_key = jnp.clip(jax.random.normal(jax.random.fold_in(key, 12), (PADROWS, full_width), jnp.float32), -8.0, 8.0) * 0.35
    return (base_query, base_key)


def draw_queries(key, part):
    return paired_rows(key)[0].astype(jnp.bfloat16)


def draw_key_rows(key, part):
    return paired_rows(key)[1].astype(jnp.bfloat16)


def draw_pair_ids(key, part):
    devices = PADROWS // CAP
    pair_count = devices // 2
    first_live = jax.random.randint(jax.random.fold_in(key, 21), (pair_count,), 0, CAP + 1)
    raw_draw = jax.random.randint(jax.random.fold_in(key, 22), (pair_count,), 0, 1 << 20)
    room_left = jnp.minimum(CAP, 2 * ROWS - first_live)
    second_live = raw_draw % (room_left + 1)
    chosen = jax.random.randint(jax.random.fold_in(key, 23), (), 0, pair_count)
    picked = jnp.arange(pair_count) == chosen
    first_live = jnp.where(picked, CAP, first_live)
    second_live = jnp.where(picked, 2 * ROWS - CAP, second_live)
    flipped = jax.random.randint(jax.random.fold_in(key, 24), (pair_count,), 0, 2) == 1
    left_live = jnp.where(flipped, second_live, first_live)
    right_live = jnp.where(flipped, first_live, second_live)
    live_rows = jnp.stack([left_live, right_live], axis=1).reshape(devices)
    cut_points = jax.random.randint(jax.random.fold_in(key, 25), (devices, SLOTS - 1), 1, CAP)
    position = jnp.arange(CAP)
    counted = jnp.sum((cut_points[:, None, :] <= position[None, :, None]).astype(jnp.int32), axis=2)
    pair_index = jnp.where(position[None, :] < live_rows[:, None], counted, SLOTS)
    return pair_index.reshape(PADROWS).astype(jnp.int32)


def steps_of(stream_key, shape, cuts, least, high):
    factor_of = 1.0
    for dim, blocks in cuts:
        steps = jax.random.uniform(jax.random.fold_in(jax.random.fold_in(stream_key, 6), dim), (blocks,), jnp.float32, least / len(cuts), high / len(cuts))
        factor_of = factor_of * jnp.repeat(jnp.exp(steps), shape[dim] // blocks).reshape((-1,) + (1,) * (len(shape) - 1 - dim))
    return factor_of


def scatter_about(stream_key, extent, deviation, reach, cuts=(), kind=jnp.bfloat16):
    values = jax.random.normal(stream_key, extent, jnp.float32) * deviation
    if len(cuts) > 0:
        values = steps_of(stream_key, extent, cuts, -0.22, 0.18) * values
    return jnp.clip(values, min=-reach, max=reach).astype(kind)


def setup_inputs(seed: int = 0) -> dict:
    streams_of = jax.random.split(jax.random.key(seed), 7)
    queries = draw_queries(jax.random.fold_in(streams_of[6], 71), 0)
    key_rows = draw_key_rows(jax.random.fold_in(streams_of[6], 71), 0)
    value_rows = scatter_about(streams_of[2], (PADROWS, HEADS * HEAD), 2.0, 12.0, ((0, 8), (1, 4)))
    pair_ids = draw_pair_ids(jax.random.fold_in(streams_of[6], 71), 0)
    out_weight = scatter_about(streams_of[4], (HEADS * HEAD, D), (HEADS * HEAD) ** -0.5, 0.09375, ((0, 4), (1, 8)))
    residual = scatter_about(streams_of[5], (TOKENS, D), 1.0, 6.0, ((0, 8), (1, 4)))
    return {"queries": queries, "key_rows": key_rows, "value_rows": value_rows, "pair_ids": pair_ids, "out_weight": out_weight, "residual": residual}


def attend_block(block):
    query_block, key_block, value_block, id_block = block
    group_size = 8 if HEADS % 8 == 0 else HEADS

    def split_heads(stacked):
        return stacked.reshape(CAP, HEADS // group_size, group_size, HEAD).transpose(1, 0, 2, 3)

    allowed = (id_block[:, None] == id_block[None, :]) & (id_block[:, None] < SLOTS)

    def per_group(operands):
        query_part, key_part, value_part = operands
        scores = jnp.einsum("qhd,khd->hqk", query_part.astype(jnp.float32), key_part.astype(jnp.float32))
        masked = jnp.where(allowed[None], scores, -1e30)
        row_top = jnp.max(masked, axis=2, keepdims=True)
        exp_terms = jnp.where(allowed[None], jnp.exp(masked - row_top), 0.0)
        row_total = jnp.maximum(jnp.sum(exp_terms, axis=2, keepdims=True), 1.0)
        weights = lax.optimization_barrier((exp_terms / row_total).astype(jnp.bfloat16))
        mixed = jnp.einsum("hqk,khd->qhd", weights.astype(jnp.float32), value_part.astype(jnp.float32))
        return mixed.astype(jnp.bfloat16)

    grouped = lax.map(per_group, (split_heads(query_block), split_heads(key_block), split_heads(value_block)))
    return grouped.transpose(1, 0, 2, 3).reshape(CAP, HEADS * HEAD)


def reference(queries, key_rows, value_rows, pair_ids, out_weight, residual):
    full_width = HEADS * HEAD
    blocks = (queries.reshape(N_PAIRS, CAP, full_width), key_rows.reshape(N_PAIRS, CAP, full_width),
              value_rows.reshape(N_PAIRS, CAP, full_width), pair_ids.reshape(N_PAIRS, CAP))
    attended = lax.map(attend_block, blocks)
    id_blocks = pair_ids.reshape(N_PAIRS, CAP)
    live_count = jnp.sum((id_blocks < SLOTS).astype(jnp.int32), axis=1)
    row_start = jnp.cumsum(live_count).astype(jnp.int32) - live_count
    position = jnp.arange(CAP, dtype=jnp.int32)
    number = row_start[:, None] + position[None, :]
    target = jnp.where(position[None, :] < live_count[:, None],
                       (number % N_PAIRS) * ROWS + number // N_PAIRS, TOKENS).astype(jnp.int32)
    moved_attended = jnp.zeros((TOKENS, full_width), jnp.bfloat16).at[target.reshape(-1)].set(
        attended.reshape(-1, full_width), mode="drop")
    group_width = full_width // N_TENSOR
    projected = jnp.zeros((TOKENS, D), jnp.float32)
    for group_index in range(N_TENSOR):
        rows_part = moved_attended[:, group_index * group_width:(group_index + 1) * group_width]
        weight_part = out_weight[group_index * group_width:(group_index + 1) * group_width, :]
        partial_value = lax.optimization_barrier(
            jnp.dot(rows_part, weight_part, preferred_element_type=jnp.float32).astype(jnp.bfloat16))
        projected = projected + partial_value.astype(jnp.float32)
    projected = lax.optimization_barrier(projected.astype(jnp.bfloat16))
    return (residual.astype(jnp.float32) + projected.astype(jnp.float32)).astype(jnp.bfloat16)
```

```python
import functools

import jax
import jax.numpy as jnp
from jax import lax
from jax.experimental import pallas as pl
from jax.experimental.pallas import tpu as pltpu
from jax.sharding import PartitionSpec as P

HEAD = 64
SLOTS = 8


def carried_in(part, axis, combine, identity):
    place = lax.axis_index(axis)
    gathered = lax.all_gather(part, axis)
    state = jnp.zeros_like(part) + jnp.asarray(identity, part.dtype)

    def one(step, state):
        return combine(state, lax.dynamic_index_in_dim(gathered, step, 0, False))

    return lax.fori_loop(0, place, one, state)


def attend_group(query_part, key_part, value_part, allowed):
    scores = jnp.einsum("qhd,khd->hqk", query_part, key_part, preferred_element_type=jnp.float32)
    masked = jnp.where(allowed[None], scores, -1e30)
    row_top = jnp.max(masked, axis=2, keepdims=True)
    exp_terms = jnp.where(allowed[None], jnp.exp(masked - row_top), 0.0)
    row_total = jnp.maximum(jnp.sum(exp_terms, axis=2, keepdims=True), 1.0)
    weights = (exp_terms / row_total).astype(jnp.bfloat16)
    mixed = jnp.einsum("hqk,khd->qhd", weights, value_part, preferred_element_type=jnp.float32)
    return mixed.astype(jnp.bfloat16)


def add_counts(earlier, later):
    return earlier + later


def shards(queries, key_rows, value_rows, pair_ids, out_weight, residual):
    cap_rows = queries.shape[0]
    local_width = queries.shape[1]
    heads_local = local_width // HEAD
    group_size = 4
    balanced_rows = residual.shape[0]
    allowed = (pair_ids[:, None] == pair_ids[None, :]) & (pair_ids[:, None] < SLOTS)

    def split_heads(stacked):
        return stacked.reshape(cap_rows, heads_local // group_size, group_size, HEAD).transpose(
            1, 0, 2, 3
        )

    def per_group(operands):
        return attend_group(operands[0], operands[1], operands[2], allowed)

    grouped = lax.map(
        per_group, (split_heads(queries), split_heads(key_rows), split_heads(value_rows))
    )
    attended = grouped.transpose(1, 0, 2, 3).reshape(cap_rows, local_width)
    live_rows = jnp.sum((pair_ids < SLOTS).astype(jnp.int32))
    devices = lax.axis_size("pairs")
    row_start = carried_in(live_rows.reshape(1), "pairs", add_counts, jnp.zeros((1,), jnp.int32))[0]
    partial_value = jnp.dot(
        attended,
        lax.all_gather(out_weight, "pairs", axis=1, tiled=True),
        preferred_element_type=jnp.float32,
    )
    payload = lax.psum_scatter(
        partial_value.astype(jnp.bfloat16), "tensor", scatter_dimension=1, tiled=True
    )
    per_peer = cap_rows // devices
    feature_width = payload.shape[1]
    peer_index = jnp.arange(devices, dtype=jnp.int32)
    turn_index = jnp.arange(per_peer, dtype=jnp.int32)
    source_rows = ((peer_index - row_start) % devices)[:, None] + devices * turn_index[None, :]
    slot_index = jnp.where(
        source_rows < live_rows, (row_start + source_rows) // devices, balanced_rows
    ).astype(jnp.int32)
    outgoing = jnp.take(payload, source_rows.reshape(-1), axis=0).reshape(
        devices, per_peer, feature_width
    )
    incoming = lax.all_to_all(outgoing, "pairs", split_axis=0, concat_axis=0, tiled=True)
    incoming_slots = lax.all_to_all(slot_index, "pairs", split_axis=0, concat_axis=0, tiled=True)
    landed = jnp.zeros((balanced_rows, feature_width), payload.dtype)
    moved_rows = landed.at[incoming_slots.reshape(-1)].set(
        incoming.reshape(-1, feature_width), mode="drop"
    )
    return (residual.astype(jnp.float32) + moved_rows.astype(jnp.float32)).astype(jnp.bfloat16)


HALVES = 2
PARTS = 2
WEIGHT_PIECES = 8
SPILL = 80
PAIR_CLASSES = 8
MESH = pl.DeviceIdType.MESH
BF16 = jnp.bfloat16
F32 = jnp.float32


def attend_pair(query_pair, key_pair, value_pair, allowed):
    low = lax.broadcasted_iota(jnp.int32, query_pair.shape, 1) < HEAD
    zero = jnp.zeros_like(query_pair)
    mixed = []
    for query_one in (jnp.where(low, query_pair, zero), jnp.where(low, zero, query_pair)):
        scores = lax.dot_general(
            query_one, key_pair, (((1,), (1,)), ((), ())), preferred_element_type=F32
        )
        masked = jnp.where(allowed, scores, -1e30)
        exp_terms = jnp.exp(masked - jnp.max(masked, axis=1, keepdims=True))
        weights = exp_terms * (1.0 / jnp.sum(exp_terms, axis=1, keepdims=True))
        mixed.append(jnp.dot(weights.astype(BF16), value_pair, preferred_element_type=F32))
    return jnp.where(low, mixed[0], mixed[1]).astype(BF16)


def class_and_turn(place, per_class):
    kind = jnp.zeros_like(place)
    for bound in range(1, PAIR_CLASSES):
        kind = kind + jnp.where(place >= bound * per_class, 1, 0)
    return kind, place - per_class * kind


def fused_kernel(
    layers, tensors,
    q_ref, k_ref, v_ref, ids_ref, w_ref, res_ref, out_ref,
    count_own, counts, w_full, attended, spilled, rows_all,
    core_out, core_in, mine, across_out, across_in, kept, summed, final_out, final_in,
    count_send, count_recv, w_send, w_recv, spill_send, spill_recv,
    own_send, relay_send, rows_recv, core_send, core_recv, across_send, across_recv,
    final_send, final_recv,
):
    devices = layers * HALVES
    cap = q_ref.shape[0]
    width = q_ref.shape[1]
    half_rows = rows_all.shape[2]
    part_width = width // PARTS
    quarter = final_in.shape[2]
    per_class = half_rows // PAIR_CLASSES
    both = HALVES * half_rows
    p = lax.axis_index("pairs")
    t = lax.axis_index("tensor")
    z = p // HALVES
    y = p % HALVES
    x = t // 2
    core = t % 2
    beside = (z * HALVES + 1 - y, t)
    other_core = (p, x * 2 + 1 - core)
    other_chip = (p, (1 - x) * 2 + core)

    barrier = pltpu.get_barrier_semaphore()
    everyone = devices * tensors

    def greet(step, carry):
        number = lax.rem(p * tensors + t + step, everyone)
        pl.semaphore_signal(
            barrier, inc=1, device_id=(number // tensors, number % tensors), device_id_type=MESH
        )
        return carry

    lax.fori_loop(1, everyone, greet, 0)

    ids_row = ids_ref[...].astype(F32)
    live = jnp.sum(jnp.where(ids_row < SLOTS, 1.0, 0.0), axis=1, keepdims=True)
    own_count = jnp.broadcast_to(live, count_own.shape).astype(jnp.int32)
    count_own[...] = own_count
    counts[p] = own_count
    w_full[y] = w_ref[...]
    ids_wide = jnp.broadcast_to(ids_row, (cap, cap))
    allowed = ids_wide == ids_wide.T
    pl.semaphore_wait(barrier, everyone - 1)

    def remote(src, dst, sent, got, where_to):
        return pltpu.make_async_remote_copy(
            src_ref=src, dst_ref=dst, send_sem=sent, recv_sem=got,
            device_id=where_to, device_id_type=MESH,
        )

    pending = []
    for step in range(1, devices):
        peer = lax.rem(p + step, devices)
        copy = remote(count_own, counts.at[p], count_send.at[step], count_recv.at[p], (peer, t))
        copy.start()
        pending.append(copy)

    piece_rows = w_ref.shape[0] // WEIGHT_PIECES

    def weight_copy(piece, slot):
        rows = pl.ds(piece * piece_rows, piece_rows)
        return remote(
            w_ref.at[rows], w_full.at[slot, rows], w_send.at[piece], w_recv.at[piece], beside
        )

    def send_weights(first, last):
        for piece in range(first, last):
            copy = weight_copy(piece, y)
            copy.start()
            pending.append(copy)

    def rows_copy(block, part, sent, layer):
        here = rows_all.at[block, part]
        return remote(here, here, sent, rows_recv.at[block, part], (layer * HALVES + y, t))

    spill_from = pl.multiple_of((1 - y) * (cap - SPILL), 16)

    def spill_copy(part):
        return remote(
            attended.at[part, pl.ds(spill_from, SPILL)], spilled.at[part],
            spill_send.at[part], spill_recv.at[part], beside,
        )

    def attend_part(part):
        for pair in range(part_width // (2 * HEAD)):
            lanes = slice(part * part_width + pair * 2 * HEAD, part * part_width + (pair + 1) * 2 * HEAD)
            attended[part, :, pair * 2 * HEAD:(pair + 1) * 2 * HEAD] = attend_pair(
                q_ref[:, lanes], k_ref[:, lanes], v_ref[:, lanes], allowed
            )
        copy = spill_copy(part)
        copy.start()
        pending.append(copy)

    send_weights(0, 1)
    attend_part(0)
    send_weights(1, 2)

    for step in range(1, devices):
        source = lax.rem(p + step, devices)
        remote(count_own, counts.at[source], count_send.at[0], count_recv.at[source], (source, t)).wait_recv()

    def start_of(block):
        total = jnp.zeros((1, cap), jnp.int32)
        for earlier in range(devices):
            total = total + jnp.where(earlier < block, counts[earlier, 0:1, :], 0)
        return total

    live_first = counts[HALVES * z, 0:1, :]
    live_second = counts[HALVES * z + 1, 0:1, :]
    second_at = both - live_second - ((both - live_first - live_second) & 7)
    start_pair = start_of(HALVES * z)
    kind, turn = class_and_turn(lax.broadcasted_iota(jnp.int32, (half_rows, cap), 0), per_class)
    slot = y * half_rows + ((kind - start_pair) & 7) + 8 * turn
    column = lax.broadcasted_iota(jnp.int32, (half_rows, cap), 1)
    row_first = slot
    row_second = slot - second_at
    row_own = jnp.where(y == 0, row_first, row_second)
    row_peer = jnp.where(y == 0, row_second, row_first)
    live_own = jnp.where(y == 0, live_first, live_second)
    live_peer = jnp.where(y == 0, live_second, live_first)
    pick_own = jnp.where((column == row_own) & (column < live_own), 1.0, 0.0).astype(BF16)
    peer_from = y * (cap - SPILL)
    pick_peer = jnp.where((column == row_peer - peer_from) & (column + peer_from < live_peer), 1.0, 0.0)
    pick_peer = pick_peer.astype(BF16)[:, :SPILL]

    def share_part(part):
        spill_copy(part).wait_recv()
        packed = jnp.dot(pick_own, attended[part], preferred_element_type=F32)
        packed = packed + jnp.dot(pick_peer, spilled[part], preferred_element_type=F32)
        rows_all[z, part] = packed.astype(BF16)

        @pl.when(z < layers - 1)
        def _():
            rows_copy(z, part, own_send.at[0, part], z + 1).start()

        @pl.when(z > 0)
        def _():
            rows_copy(z, part, own_send.at[1, part], z - 1).start()

    share_part(0)
    for part in range(1, PARTS):
        attend_part(part)
        share_part(part)
    send_weights(2, WEIGHT_PIECES)

    order = (
        z,
        jnp.where(z % 2 == 0, z + 1, z - 1),
        jnp.where(z < 2, 2, 1),
        jnp.where(z < 2, 3, 0),
    )
    inner = (z > 0) & (z < layers - 1)

    def take_rows(turn_index, relay):
        block = order[turn_index]
        onward = jnp.where(block < z, z + 1, z - 1)
        for part in range(PARTS):
            copy = rows_copy(block, part, relay_send.at[turn_index, part], onward)
            copy.wait_recv()
            if relay:
                copy.start()

    def take_and_relay(turn_index):
        @pl.when(inner)
        def _():
            take_rows(turn_index, True)

    def take_last(turn_index):
        @pl.when(jnp.logical_not(inner))
        def _():
            take_rows(turn_index, False)

    def partial_of(turn_index, side):
        block = order[turn_index]
        total = jnp.zeros((half_rows, w_ref.shape[1]), F32)
        for part in range(PARTS):
            total = total + jnp.dot(
                rows_all[block, part],
                w_full[side, part * part_width:(part + 1) * part_width, :],
                preferred_element_type=F32,
            )
        return total

    def core_copy(turn_index):
        return remote(
            core_out.at[turn_index], core_in.at[turn_index],
            core_send.at[turn_index], core_recv.at[turn_index], other_core,
        )

    def across_copy(turn_index):
        return remote(
            across_out.at[turn_index], across_in.at[turn_index],
            across_send.at[turn_index], across_recv.at[turn_index], other_chip,
        )

    def multiply(turn_index):
        core_out[turn_index] = partial_of(turn_index, 1 - core).astype(BF16)
        copy = core_copy(turn_index)
        copy.start()
        pending.append(copy)
        mine[turn_index] = partial_of(turn_index, core).astype(BF16)

    def add_cores(turn_index):
        core_copy(turn_index).wait_recv()
        total = mine[turn_index].astype(F32) + core_in[turn_index].astype(F32)
        left, right = total[:, :quarter], total[:, quarter:]
        across_out[turn_index] = jnp.where(x == 0, right, left).astype(BF16)
        kept[turn_index] = jnp.where(x == 0, left, right)
        copy = across_copy(turn_index)
        copy.start()
        pending.append(copy)

    def add_chips(turn_index):
        across_copy(turn_index).wait_recv()
        total = kept[turn_index] + across_in[turn_index].astype(F32)
        summed[:, order[turn_index]] = total.reshape(PAIR_CLASSES, per_class, quarter)

    take_and_relay(1)
    take_and_relay(2)
    take_and_relay(3)
    take_last(1)
    take_last(2)
    for piece in range(WEIGHT_PIECES):
        weight_copy(piece, 1 - y).wait_recv()
    for turn_index in range(layers - 1):
        multiply(turn_index)
        if turn_index > 0:
            add_cores(turn_index - 1)
    add_cores(layers - 2)
    take_last(3)
    multiply(layers - 1)
    add_cores(layers - 1)
    for turn_index in range(layers):
        add_chips(turn_index)

    final_out[...] = summed[...].reshape(final_out.shape).astype(BF16)
    source_slot = y * tensors + core * 2 + x
    to_self = z == t

    def final_copy(step):
        peer = lax.rem(p + step, devices)
        return remote(
            final_out.at[peer], final_in.at[source_slot],
            final_send.at[step], final_recv.at[source_slot], (peer, z),
        )

    for step in range(1, devices):
        copy = final_copy(step)
        copy.start()
        pending.append(copy)

    @pl.when(to_self)
    def _():
        final_in[source_slot] = final_out[p]

    @pl.when(jnp.logical_not(to_self))
    def _():
        final_copy(0).start()

    place_shape = (half_rows, HALVES * layers * per_class)
    lane = lax.broadcasted_iota(jnp.int32, (1, place_shape[1]), 1)
    side = jnp.where(lane >= layers * per_class, 1, 0)
    lane = lane - side * layers * per_class
    layer = jnp.zeros_like(lane)
    for bound in range(1, layers):
        layer = layer + jnp.where(lane >= bound * per_class, 1, 0)
    lane = lane - layer * per_class
    spot = jnp.zeros_like(lane) - 1
    count_width = place_shape[1]
    for block in range(layers):
        first = counts[HALVES * block, 0:1, :][:, :count_width]
        second = counts[HALVES * block + 1, 0:1, :][:, :count_width]
        begin = start_of(HALVES * block)[:, :count_width]
        second_from = both - second - ((both - first - second) & 7)
        where_at = side * half_rows + ((p - begin) & 7) + 8 * lane
        number = jnp.where(
            where_at < first, begin + where_at,
            jnp.where(
                (where_at >= second_from) & (where_at < second_from + second),
                begin + first + where_at - second_from, -8,
            ),
        )
        spot = jnp.where(layer == block, number >> 3, spot)
    place = jnp.where(
        lax.broadcasted_iota(jnp.int32, place_shape, 0) == spot, 1.0, 0.0
    ).astype(BF16)

    for half in range(HALVES):
        for piece in range(tensors):
            slot_index = half * tensors + piece
            from_self = (z == t) & (source_slot == slot_index)

            @pl.when(jnp.logical_not(from_self))
            def _():
                remote(
                    final_out.at[0], final_in.at[slot_index], final_send.at[0],
                    final_recv.at[slot_index], (lax.rem(p + 1, devices), t),
                ).wait_recv()

    depth = layers * per_class
    for piece in range(tensors):
        columns = slice(piece * quarter, (piece + 1) * quarter)
        moved = res_ref[:, columns].astype(F32)
        for half in range(HALVES):
            moved = moved + jnp.dot(
                place[:, half * depth:(half + 1) * depth],
                final_in[half * tensors + piece], preferred_element_type=F32,
            )
        out_ref[:, columns] = moved.astype(BF16)

    for copy in pending:
        copy.wait_send()
    for part in range(PARTS):
        @pl.when(z < layers - 1)
        def _():
            rows_copy(z, part, own_send.at[0, part], z + 1).wait_send()

        @pl.when(z > 0)
        def _():
            rows_copy(z, part, own_send.at[1, part], z - 1).wait_send()

    @pl.when(inner)
    def _():
        for turn_index in range(1, layers):
            block = order[turn_index]
            onward = jnp.where(block < z, z + 1, z - 1)
            for part in range(PARTS):
                rows_copy(block, part, relay_send.at[turn_index, part], onward).wait_send()

    @pl.when(jnp.logical_not(to_self))
    def _():
        final_copy(0).wait_send()


def fused_shards(layers, tensors, queries, key_rows, value_rows, pair_ids, out_weight, residual):
    devices = layers * HALVES
    cap, width = queries.shape
    half_rows = residual.shape[0]
    columns = out_weight.shape[1]
    quarter = columns // 2
    part_width = width // PARTS
    per_class = half_rows // PAIR_CLASSES
    depth = layers * per_class
    dma = pltpu.SemaphoreType.DMA
    vmem = pltpu.VMEM
    scratch = [
        vmem((8, cap), jnp.int32),
        vmem((devices, 8, cap), jnp.int32),
        vmem((HALVES, width, columns), BF16),
        vmem((PARTS, cap, part_width), BF16),
        vmem((PARTS, SPILL, part_width), BF16),
        vmem((layers, PARTS, half_rows, part_width), BF16),
        vmem((layers, half_rows, columns), BF16),
        vmem((layers, half_rows, columns), BF16),
        vmem((layers, half_rows, columns), BF16),
        vmem((layers, half_rows, quarter), BF16),
        vmem((layers, half_rows, quarter), BF16),
        vmem((layers, half_rows, quarter), F32),
        vmem((PAIR_CLASSES, layers, per_class, quarter), F32),
        vmem((devices, depth, quarter), BF16),
        vmem((HALVES * tensors, depth, quarter), BF16),
        dma((devices,)), dma((devices,)),
        dma((WEIGHT_PIECES,)), dma((WEIGHT_PIECES,)),
        dma((PARTS,)), dma((PARTS,)),
        dma((2, PARTS)), dma((layers, PARTS)), dma((layers, PARTS)),
        dma((layers,)), dma((layers,)),
        dma((layers,)), dma((layers,)),
        dma((devices,)), dma((HALVES * tensors,)),
    ]
    in_vmem = pl.BlockSpec(memory_space=pltpu.VMEM)
    return pl.pallas_call(
        functools.partial(fused_kernel, layers, tensors),
        out_shape=jax.ShapeDtypeStruct(residual.shape, residual.dtype),
        in_specs=[in_vmem] * 6,
        out_specs=in_vmem,
        scratch_shapes=scratch,
        compiler_params=pltpu.CompilerParams(
            collective_id=0, has_side_effects=True, vmem_limit_bytes=48 * 1024 * 1024
        ),
    )(queries, key_rows, value_rows, pair_ids.reshape(1, cap), out_weight, residual)


def fits_fused(mesh):
    layers = mesh.shape["pairs"] // HALVES
    return mesh.shape["tensor"] == 4 and layers == 4


def solution(mesh):
    in_specs = (
        P("pairs", "tensor"),
        P("pairs", "tensor"),
        P("pairs", "tensor"),
        P("pairs"),
        P("tensor", "pairs"),
        P("pairs", "tensor"),
    )
    out_specs = P("pairs", "tensor")
    per_device = shards
    if fits_fused(mesh):
        per_device = functools.partial(fused_shards, mesh.shape["pairs"] // HALVES, mesh.shape["tensor"])
    return jax.shard_map(per_device, mesh=mesh, in_specs=in_specs, out_specs=out_specs, check_vma=False)
```

```python
import functools

import jax
import jax.numpy as jnp
from jax import lax
from jax.experimental import pallas as pl
from jax.experimental.pallas import tpu as pltpu
from jax.sharding import PartitionSpec as P

HEAD = 64
SLOTS = 8


def carried_in(part, axis, combine, identity):
    place = lax.axis_index(axis)
    gathered = lax.all_gather(part, axis)
    state = jnp.zeros_like(part) + jnp.asarray(identity, part.dtype)

    def one(step, state):
        return combine(state, lax.dynamic_index_in_dim(gathered, step, 0, False))

    return lax.fori_loop(0, place, one, state)


def attend_group(query_part, key_part, value_part, allowed):
    scores = jnp.einsum("qhd,khd->hqk", query_part, key_part, preferred_element_type=jnp.float32)
    masked = jnp.where(allowed[None], scores, -1e30)
    row_top = jnp.max(masked, axis=2, keepdims=True)
    exp_terms = jnp.where(allowed[None], jnp.exp(masked - row_top), 0.0)
    row_total = jnp.maximum(jnp.sum(exp_terms, axis=2, keepdims=True), 1.0)
    weights = (exp_terms / row_total).astype(jnp.bfloat16)
    mixed = jnp.einsum("hqk,khd->qhd", weights, value_part, preferred_element_type=jnp.float32)
    return mixed.astype(jnp.bfloat16)


def add_counts(earlier, later):
    return earlier + later


def shards(queries, key_rows, value_rows, pair_ids, out_weight, residual):
    cap_rows = queries.shape[0]
    local_width = queries.shape[1]
    heads_local = local_width // HEAD
    group_size = 4
    balanced_rows = residual.shape[0]
    allowed = (pair_ids[:, None] == pair_ids[None, :]) & (pair_ids[:, None] < SLOTS)

    def split_heads(stacked):
        return stacked.reshape(cap_rows, heads_local // group_size, group_size, HEAD).transpose(
            1, 0, 2, 3
        )

    def per_group(operands):
        return attend_group(operands[0], operands[1], operands[2], allowed)

    grouped = lax.map(
        per_group, (split_heads(queries), split_heads(key_rows), split_heads(value_rows))
    )
    attended = grouped.transpose(1, 0, 2, 3).reshape(cap_rows, local_width)
    live_rows = jnp.sum((pair_ids < SLOTS).astype(jnp.int32))
    devices = lax.axis_size("pairs")
    row_start = carried_in(live_rows.reshape(1), "pairs", add_counts, jnp.zeros((1,), jnp.int32))[0]
    partial_value = jnp.dot(
        attended,
        lax.all_gather(out_weight, "pairs", axis=1, tiled=True),
        preferred_element_type=jnp.float32,
    )
    payload = lax.psum_scatter(
        partial_value.astype(jnp.bfloat16), "tensor", scatter_dimension=1, tiled=True
    )
    per_peer = cap_rows // devices
    feature_width = payload.shape[1]
    peer_index = jnp.arange(devices, dtype=jnp.int32)
    turn_index = jnp.arange(per_peer, dtype=jnp.int32)
    source_rows = ((peer_index - row_start) % devices)[:, None] + devices * turn_index[None, :]
    slot_index = jnp.where(
        source_rows < live_rows, (row_start + source_rows) // devices, balanced_rows
    ).astype(jnp.int32)
    outgoing = jnp.take(payload, source_rows.reshape(-1), axis=0).reshape(
        devices, per_peer, feature_width
    )
    incoming = lax.all_to_all(outgoing, "pairs", split_axis=0, concat_axis=0, tiled=True)
    incoming_slots = lax.all_to_all(slot_index, "pairs", split_axis=0, concat_axis=0, tiled=True)
    landed = jnp.zeros((balanced_rows, feature_width), payload.dtype)
    moved_rows = landed.at[incoming_slots.reshape(-1)].set(
        incoming.reshape(-1, feature_width), mode="drop"
    )
    return (residual.astype(jnp.float32) + moved_rows.astype(jnp.float32)).astype(jnp.bfloat16)


HALVES = 2
PARTS = 4
WEIGHT_PIECES = 8
SPILL = 80
PAIR_CLASSES = 8
MESH = pl.DeviceIdType.MESH
BF16 = jnp.bfloat16
F32 = jnp.float32


def attend_pair(query_pair, key_pair, value_pair, allowed):
    low = lax.broadcasted_iota(jnp.int32, query_pair.shape, 1) < HEAD
    zero = jnp.zeros_like(query_pair)
    mixed = []
    for query_one in (jnp.where(low, query_pair, zero), jnp.where(low, zero, query_pair)):
        scores = lax.dot_general(
            query_one, key_pair, (((1,), (1,)), ((), ())), preferred_element_type=F32
        )
        masked = jnp.where(allowed, scores, -1e30)
        exp_terms = jnp.exp(masked - jnp.max(masked, axis=1, keepdims=True))
        weights = exp_terms * (1.0 / jnp.sum(exp_terms, axis=1, keepdims=True))
        mixed.append(jnp.dot(weights.astype(BF16), value_pair, preferred_element_type=F32))
    return jnp.where(low, mixed[0], mixed[1]).astype(BF16)


def class_and_turn(place, per_class):
    kind = jnp.zeros_like(place)
    for bound in range(1, PAIR_CLASSES):
        kind = kind + jnp.where(place >= bound * per_class, 1, 0)
    return kind, place - per_class * kind


def fused_kernel(
    layers, tensors,
    q_hbm, k_hbm, v_hbm, ids_hbm, w_ref, res_hbm, out_ref,
    q_ref, k_ref, v_ref, ids_ref, res_ref,
    count_own, counts, w_full, attended, spilled, rows_all,
    core_out, core_in, mine, across_out, across_in, kept, summed, final_out, final_in,
    count_send, count_recv, w_send, w_recv, spill_send, spill_recv,
    own_send, relay_send, rows_recv, core_send, core_recv, across_send, across_recv,
    final_send, final_recv, load_sem, ids_sem, w_sem, res_sem,
):
    devices = layers * HALVES
    cap = q_ref.shape[0]
    width = q_ref.shape[1]
    half_rows = rows_all.shape[2]
    part_width = width // PARTS
    quarter = final_in.shape[2]
    per_class = half_rows // PAIR_CLASSES
    both = HALVES * half_rows
    p = lax.axis_index("pairs")
    t = lax.axis_index("tensor")
    z = p // HALVES
    y = p % HALVES
    x = t // 2
    core = t % 2
    beside = (z * HALVES + 1 - y, t)
    other_core = (p, x * 2 + 1 - core)
    other_chip = (p, (1 - x) * 2 + core)

    barrier = pltpu.get_barrier_semaphore()
    everyone = devices * tensors

    def greet(step, carry):
        number = lax.rem(p * tensors + t + step, everyone)
        pl.semaphore_signal(
            barrier, inc=1, device_id=(number // tensors, number % tensors), device_id_type=MESH
        )
        return carry

    loads = {}
    ids_load = pltpu.make_async_copy(ids_hbm, ids_ref, ids_sem)
    ids_load.start()
    for part in range(PARTS):
        columns = slice(part * part_width, (part + 1) * part_width)
        for which, (src, dst) in enumerate(((q_hbm, q_ref), (k_hbm, k_ref), (v_hbm, v_ref))):
            loads[part, which] = pltpu.make_async_copy(
                src.at[:, columns], dst.at[:, columns], load_sem.at[part, which]
            )
            loads[part, which].start()
    w_load = pltpu.make_async_copy(w_ref, w_full.at[y], w_sem)
    w_load.start()
    res_load = pltpu.make_async_copy(res_hbm, res_ref, res_sem)
    res_load.start()

    lax.fori_loop(1, everyone, greet, 0)
    ids_load.wait()

    ids_row = ids_ref[...].astype(F32)
    live = jnp.sum(jnp.where(ids_row < SLOTS, 1.0, 0.0), axis=1, keepdims=True)
    own_count = jnp.broadcast_to(live, count_own.shape).astype(jnp.int32)
    count_own[...] = own_count
    counts[p] = own_count
    ids_wide = jnp.broadcast_to(ids_row, (cap, cap))
    allowed = ids_wide == ids_wide.T
    pl.semaphore_wait(barrier, everyone - 1)

    def remote(src, dst, sent, got, where_to):
        return pltpu.make_async_remote_copy(
            src_ref=src, dst_ref=dst, send_sem=sent, recv_sem=got,
            device_id=where_to, device_id_type=MESH,
        )

    pending = []
    for step in range(1, devices):
        peer = lax.rem(p + step, devices)
        copy = remote(count_own, counts.at[p], count_send.at[step], count_recv.at[p], (peer, t))
        copy.start()
        pending.append(copy)

    piece_rows = w_ref.shape[0] // WEIGHT_PIECES

    def weight_copy(piece, slot):
        rows = pl.ds(piece * piece_rows, piece_rows)
        return remote(
            w_ref.at[rows], w_full.at[slot, rows], w_send.at[piece], w_recv.at[piece], beside
        )

    def send_weights(first, last):
        for piece in range(first, last):
            copy = weight_copy(piece, y)
            copy.start()
            pending.append(copy)

    def rows_copy(block, part, sent, layer):
        here = rows_all.at[block, part]
        return remote(here, here, sent, rows_recv.at[block, part], (layer * HALVES + y, t))

    spill_from = pl.multiple_of((1 - y) * (cap - SPILL), 16)

    def spill_copy(part):
        return remote(
            attended.at[part, pl.ds(spill_from, SPILL)], spilled.at[part],
            spill_send.at[part], spill_recv.at[part], beside,
        )

    def attend_part(part):
        for which in range(3):
            loads[part, which].wait()
        for pair in range(part_width // (2 * HEAD)):
            lanes = slice(part * part_width + pair * 2 * HEAD, part * part_width + (pair + 1) * 2 * HEAD)
            attended[part, :, pair * 2 * HEAD:(pair + 1) * 2 * HEAD] = attend_pair(
                q_ref[:, lanes], k_ref[:, lanes], v_ref[:, lanes], allowed
            )
        copy = spill_copy(part)
        copy.start()
        pending.append(copy)

    send_weights(0, 1)
    attend_part(0)
    send_weights(1, 2)

    for step in range(1, devices):
        source = lax.rem(p + step, devices)
        remote(count_own, counts.at[source], count_send.at[0], count_recv.at[source], (source, t)).wait_recv()

    def start_of(block):
        total = jnp.zeros((1, cap), jnp.int32)
        for earlier in range(devices):
            total = total + jnp.where(earlier < block, counts[earlier, 0:1, :], 0)
        return total

    live_first = counts[HALVES * z, 0:1, :]
    live_second = counts[HALVES * z + 1, 0:1, :]
    second_at = both - live_second - ((both - live_first - live_second) & 7)
    start_pair = start_of(HALVES * z)
    kind, turn = class_and_turn(lax.broadcasted_iota(jnp.int32, (half_rows, cap), 0), per_class)
    slot = y * half_rows + ((kind - start_pair) & 7) + 8 * turn
    column = lax.broadcasted_iota(jnp.int32, (half_rows, cap), 1)
    row_first = slot
    row_second = slot - second_at
    row_own = jnp.where(y == 0, row_first, row_second)
    row_peer = jnp.where(y == 0, row_second, row_first)
    live_own = jnp.where(y == 0, live_first, live_second)
    live_peer = jnp.where(y == 0, live_second, live_first)
    pick_own = jnp.where((column == row_own) & (column < live_own), 1.0, 0.0).astype(BF16)
    peer_from = y * (cap - SPILL)
    pick_peer = jnp.where((column == row_peer - peer_from) & (column + peer_from < live_peer), 1.0, 0.0)
    pick_peer = pick_peer.astype(BF16)[:, :SPILL]

    def share_part(part):
        spill_copy(part).wait_recv()
        packed = jnp.dot(pick_own, attended[part], preferred_element_type=F32)
        packed = packed + jnp.dot(pick_peer, spilled[part], preferred_element_type=F32)
        rows_all[z, part] = packed.astype(BF16)

        @pl.when(z < layers - 1)
        def _():
            rows_copy(z, part, own_send.at[0, part], z + 1).start()

        @pl.when(z > 0)
        def _():
            rows_copy(z, part, own_send.at[1, part], z - 1).start()

    share_part(0)
    for part in range(1, PARTS):
        attend_part(part)
        share_part(part)
    send_weights(2, WEIGHT_PIECES)

    order = (
        z,
        jnp.where(z % 2 == 0, z + 1, z - 1),
        jnp.where(z < 2, 2, 1),
        jnp.where(z < 2, 3, 0),
    )
    inner = (z > 0) & (z < layers - 1)

    def take_rows(turn_index, relay):
        block = order[turn_index]
        onward = jnp.where(block < z, z + 1, z - 1)
        for part in range(PARTS):
            copy = rows_copy(block, part, relay_send.at[turn_index, part], onward)
            copy.wait_recv()
            if relay:
                copy.start()

    def take_inner(turn_index):
        @pl.when(inner)
        def _():
            take_rows(turn_index, True)

    def take_outer(turn_index):
        @pl.when(jnp.logical_not(inner))
        def _():
            take_rows(turn_index, False)

    def partial_of(turn_index, side):
        block = order[turn_index]
        total = jnp.zeros((half_rows, w_ref.shape[1]), F32)
        for part in range(PARTS):
            total = total + jnp.dot(
                rows_all[block, part],
                w_full[side, part * part_width:(part + 1) * part_width, :],
                preferred_element_type=F32,
            )
        return total

    def core_copy(turn_index):
        return remote(
            core_out.at[turn_index], core_in.at[turn_index],
            core_send.at[turn_index], core_recv.at[turn_index], other_core,
        )

    def across_copy(turn_index):
        return remote(
            across_out.at[turn_index], across_in.at[turn_index],
            across_send.at[turn_index], across_recv.at[turn_index], other_chip,
        )

    def multiply(turn_index, side):
        value = partial_of(turn_index, side).astype(BF16)

        @pl.when(core == side)
        def _():
            mine[turn_index] = value

        @pl.when(core != side)
        def _():
            core_out[turn_index] = value
            core_copy(turn_index).start()

    def add_cores(turn_index):
        core_copy(turn_index).wait_recv()
        total = mine[turn_index].astype(F32) + core_in[turn_index].astype(F32)
        left, right = total[:, :quarter], total[:, quarter:]
        across_out[turn_index] = jnp.where(x == 0, right, left).astype(BF16)
        kept[turn_index] = jnp.where(x == 0, left, right)
        across_copy(turn_index).start()

    def add_chips(turn_index):
        across_copy(turn_index).wait_recv()
        total = kept[turn_index] + across_in[turn_index].astype(F32)
        summed[:, order[turn_index]] = total.reshape(PAIR_CLASSES, per_class, quarter)

    last = layers - 1
    w_load.wait()
    multiply(0, y)
    for turn_index in range(1, last):
        take_inner(turn_index)
        take_outer(turn_index)
        multiply(turn_index, y)

        @pl.when(core == y)
        def _():
            add_cores(turn_index - 1)

    take_inner(last)
    for piece in range(WEIGHT_PIECES):
        weight_copy(piece, 1 - y).wait_recv()

    @pl.when(core == y)
    def _():
        add_cores(last - 1)

    for turn_index in range(last):
        multiply(turn_index, 1 - y)

        @pl.when(core != y)
        def _():
            add_cores(turn_index)

    take_outer(last)
    multiply(last, y)
    multiply(last, 1 - y)
    add_cores(last)
    for turn_index in range(layers):
        add_chips(turn_index)

    final_out[...] = summed[...].reshape(final_out.shape).astype(BF16)
    source_slot = y * tensors + core * 2 + x
    to_self = z == t

    def final_copy(step):
        peer = lax.rem(p + step, devices)
        return remote(
            final_out.at[peer], final_in.at[source_slot],
            final_send.at[step], final_recv.at[source_slot], (peer, z),
        )

    for step in range(1, devices):
        copy = final_copy(step)
        copy.start()
        pending.append(copy)

    @pl.when(to_self)
    def _():
        final_in[source_slot] = final_out[p]

    @pl.when(jnp.logical_not(to_self))
    def _():
        final_copy(0).start()

    place_shape = (half_rows, HALVES * layers * per_class)
    lane = lax.broadcasted_iota(jnp.int32, (1, place_shape[1]), 1)
    side = jnp.where(lane >= layers * per_class, 1, 0)
    lane = lane - side * layers * per_class
    layer = jnp.zeros_like(lane)
    for bound in range(1, layers):
        layer = layer + jnp.where(lane >= bound * per_class, 1, 0)
    lane = lane - layer * per_class
    spot = jnp.zeros_like(lane) - 1
    count_width = place_shape[1]
    for block in range(layers):
        first = counts[HALVES * block, 0:1, :][:, :count_width]
        second = counts[HALVES * block + 1, 0:1, :][:, :count_width]
        begin = start_of(HALVES * block)[:, :count_width]
        second_from = both - second - ((both - first - second) & 7)
        where_at = side * half_rows + ((p - begin) & 7) + 8 * lane
        number = jnp.where(
            where_at < first, begin + where_at,
            jnp.where(
                (where_at >= second_from) & (where_at < second_from + second),
                begin + first + where_at - second_from, -8,
            ),
        )
        spot = jnp.where(layer == block, number >> 3, spot)
    place = jnp.where(
        lax.broadcasted_iota(jnp.int32, place_shape, 0) == spot, 1.0, 0.0
    ).astype(BF16)

    for half in range(HALVES):
        for piece in range(tensors):
            slot_index = half * tensors + piece
            from_self = (z == t) & (source_slot == slot_index)

            @pl.when(jnp.logical_not(from_self))
            def _():
                remote(
                    final_out.at[0], final_in.at[slot_index], final_send.at[0],
                    final_recv.at[slot_index], (lax.rem(p + 1, devices), t),
                ).wait_recv()

    res_load.wait()
    depth = layers * per_class
    for piece in range(tensors):
        columns = slice(piece * quarter, (piece + 1) * quarter)
        moved = res_ref[:, columns].astype(F32)
        for half in range(HALVES):
            moved = moved + jnp.dot(
                place[:, half * depth:(half + 1) * depth],
                final_in[half * tensors + piece], preferred_element_type=F32,
            )
        out_ref[:, columns] = moved.astype(BF16)

    for copy in pending:
        copy.wait_send()
    for turn_index in range(layers):
        core_copy(turn_index).wait_send()
        across_copy(turn_index).wait_send()
    for part in range(PARTS):
        @pl.when(z < layers - 1)
        def _():
            rows_copy(z, part, own_send.at[0, part], z + 1).wait_send()

        @pl.when(z > 0)
        def _():
            rows_copy(z, part, own_send.at[1, part], z - 1).wait_send()

    @pl.when(inner)
    def _():
        for turn_index in range(1, layers):
            block = order[turn_index]
            onward = jnp.where(block < z, z + 1, z - 1)
            for part in range(PARTS):
                rows_copy(block, part, relay_send.at[turn_index, part], onward).wait_send()

    @pl.when(jnp.logical_not(to_self))
    def _():
        final_copy(0).wait_send()


def fused_shards(layers, tensors, queries, key_rows, value_rows, pair_ids, out_weight, residual):
    devices = layers * HALVES
    cap, width = queries.shape
    half_rows = residual.shape[0]
    columns = out_weight.shape[1]
    quarter = columns // 2
    part_width = width // PARTS
    per_class = half_rows // PAIR_CLASSES
    depth = layers * per_class
    dma = pltpu.SemaphoreType.DMA
    vmem = pltpu.VMEM
    scratch = [
        vmem((cap, width), BF16), vmem((cap, width), BF16), vmem((cap, width), BF16),
        vmem((1, cap), jnp.int32),
        vmem(residual.shape, BF16),
        vmem((8, cap), jnp.int32),
        vmem((devices, 8, cap), jnp.int32),
        vmem((HALVES, width, columns), BF16),
        vmem((PARTS, cap, part_width), BF16),
        vmem((PARTS, SPILL, part_width), BF16),
        vmem((layers, PARTS, half_rows, part_width), BF16),
        vmem((layers, half_rows, columns), BF16),
        vmem((layers, half_rows, columns), BF16),
        vmem((layers, half_rows, columns), BF16),
        vmem((layers, half_rows, quarter), BF16),
        vmem((layers, half_rows, quarter), BF16),
        vmem((layers, half_rows, quarter), F32),
        vmem((PAIR_CLASSES, layers, per_class, quarter), F32),
        vmem((devices, depth, quarter), BF16),
        vmem((HALVES * tensors, depth, quarter), BF16),
        dma((devices,)), dma((devices,)),
        dma((WEIGHT_PIECES,)), dma((WEIGHT_PIECES,)),
        dma((PARTS,)), dma((PARTS,)),
        dma((2, PARTS)), dma((layers, PARTS)), dma((layers, PARTS)),
        dma((layers,)), dma((layers,)),
        dma((layers,)), dma((layers,)),
        dma((devices,)), dma((HALVES * tensors,)),
        dma((PARTS, 3)), dma, dma, dma,
    ]
    in_vmem = pl.BlockSpec(memory_space=pltpu.VMEM)
    return pl.pallas_call(
        functools.partial(fused_kernel, layers, tensors),
        out_shape=jax.ShapeDtypeStruct(residual.shape, residual.dtype),
        in_specs=[pl.BlockSpec(memory_space=pl.ANY)] * 6,
        out_specs=in_vmem,
        scratch_shapes=scratch,
        compiler_params=pltpu.CompilerParams(
            collective_id=0, has_side_effects=True, vmem_limit_bytes=56 * 1024 * 1024
        ),
    )(queries, key_rows, value_rows, pair_ids.reshape(1, cap), out_weight, residual)


def fits_fused(mesh):
    layers = mesh.shape["pairs"] // HALVES
    return mesh.shape["tensor"] == 4 and layers == 4


def solution(mesh):
    in_specs = (
        P("pairs", "tensor"),
        P("pairs", "tensor"),
        P("pairs", "tensor"),
        P("pairs"),
        P("tensor", "pairs"),
        P("pairs", "tensor"),
    )
    out_specs = P("pairs", "tensor")
    per_device = shards
    if fits_fused(mesh):
        per_device = functools.partial(fused_shards, mesh.shape["pairs"] // HALVES, mesh.shape["tensor"])
    return jax.shard_map(per_device, mesh=mesh, in_specs=in_specs, out_specs=out_specs, check_vma=False)
```

```python
import functools

import jax
import jax.numpy as jnp
from jax import lax
from jax.experimental import pallas as pl
from jax.experimental.pallas import tpu as pltpu
from jax.sharding import PartitionSpec as P

HEAD = 64
SLOTS = 8


def carried_in(part, axis, combine, identity):
    place = lax.axis_index(axis)
    gathered = lax.all_gather(part, axis)
    state = jnp.zeros_like(part) + jnp.asarray(identity, part.dtype)

    def one(step, state):
        return combine(state, lax.dynamic_index_in_dim(gathered, step, 0, False))

    return lax.fori_loop(0, place, one, state)


def attend_group(query_part, key_part, value_part, allowed):
    scores = jnp.einsum("qhd,khd->hqk", query_part, key_part, preferred_element_type=jnp.float32)
    masked = jnp.where(allowed[None], scores, -1e30)
    row_top = jnp.max(masked, axis=2, keepdims=True)
    exp_terms = jnp.where(allowed[None], jnp.exp(masked - row_top), 0.0)
    row_total = jnp.maximum(jnp.sum(exp_terms, axis=2, keepdims=True), 1.0)
    weights = (exp_terms / row_total).astype(jnp.bfloat16)
    mixed = jnp.einsum("hqk,khd->qhd", weights, value_part, preferred_element_type=jnp.float32)
    return mixed.astype(jnp.bfloat16)


def add_counts(earlier, later):
    return earlier + later


def shards(queries, key_rows, value_rows, pair_ids, out_weight, residual):
    cap_rows = queries.shape[0]
    local_width = queries.shape[1]
    heads_local = local_width // HEAD
    group_size = 4
    balanced_rows = residual.shape[0]
    allowed = (pair_ids[:, None] == pair_ids[None, :]) & (pair_ids[:, None] < SLOTS)

    def split_heads(stacked):
        return stacked.reshape(cap_rows, heads_local // group_size, group_size, HEAD).transpose(
            1, 0, 2, 3
        )

    def per_group(operands):
        return attend_group(operands[0], operands[1], operands[2], allowed)

    grouped = lax.map(
        per_group, (split_heads(queries), split_heads(key_rows), split_heads(value_rows))
    )
    attended = grouped.transpose(1, 0, 2, 3).reshape(cap_rows, local_width)
    live_rows = jnp.sum((pair_ids < SLOTS).astype(jnp.int32))
    devices = lax.axis_size("pairs")
    row_start = carried_in(live_rows.reshape(1), "pairs", add_counts, jnp.zeros((1,), jnp.int32))[0]
    partial_value = jnp.dot(
        attended,
        lax.all_gather(out_weight, "pairs", axis=1, tiled=True),
        preferred_element_type=jnp.float32,
    )
    payload = lax.psum_scatter(
        partial_value.astype(jnp.bfloat16), "tensor", scatter_dimension=1, tiled=True
    )
    per_peer = cap_rows // devices
    feature_width = payload.shape[1]
    peer_index = jnp.arange(devices, dtype=jnp.int32)
    turn_index = jnp.arange(per_peer, dtype=jnp.int32)
    source_rows = ((peer_index - row_start) % devices)[:, None] + devices * turn_index[None, :]
    slot_index = jnp.where(
        source_rows < live_rows, (row_start + source_rows) // devices, balanced_rows
    ).astype(jnp.int32)
    outgoing = jnp.take(payload, source_rows.reshape(-1), axis=0).reshape(
        devices, per_peer, feature_width
    )
    incoming = lax.all_to_all(outgoing, "pairs", split_axis=0, concat_axis=0, tiled=True)
    incoming_slots = lax.all_to_all(slot_index, "pairs", split_axis=0, concat_axis=0, tiled=True)
    landed = jnp.zeros((balanced_rows, feature_width), payload.dtype)
    moved_rows = landed.at[incoming_slots.reshape(-1)].set(
        incoming.reshape(-1, feature_width), mode="drop"
    )
    return (residual.astype(jnp.float32) + moved_rows.astype(jnp.float32)).astype(jnp.bfloat16)


HALVES = 2
PARTS = 4
WEIGHT_PIECES = 8
SPILL = 80
BATCHES = 2
PAIR_CLASSES = 8
MESH = pl.DeviceIdType.MESH
BF16 = jnp.bfloat16
F32 = jnp.float32


def attend_pair(query_pair, key_pair, value_pair, allowed):
    low = lax.broadcasted_iota(jnp.int32, query_pair.shape, 1) < HEAD
    zero = jnp.zeros_like(query_pair)
    mixed = []
    for query_one in (jnp.where(low, query_pair, zero), jnp.where(low, zero, query_pair)):
        scores = lax.dot_general(
            query_one, key_pair, (((1,), (1,)), ((), ())), preferred_element_type=F32
        )
        masked = jnp.where(allowed, scores, -1e30)
        exp_terms = jnp.exp(masked - jnp.max(masked, axis=1, keepdims=True))
        weights = exp_terms * (1.0 / jnp.sum(exp_terms, axis=1, keepdims=True))
        mixed.append(jnp.dot(weights.astype(BF16), value_pair, preferred_element_type=F32))
    return jnp.where(low, mixed[0], mixed[1]).astype(BF16)


def class_and_turn(place, per_class):
    kind = jnp.zeros_like(place)
    for bound in range(1, PAIR_CLASSES):
        kind = kind + jnp.where(place >= bound * per_class, 1, 0)
    return kind, place - per_class * kind


def fused_kernel(
    layers, tensors,
    q_hbm, k_hbm, v_hbm, ids_hbm, w_ref, res_hbm, out_ref,
    q_ref, k_ref, v_ref, ids_ref, res_ref,
    count_own, counts, w_full, attended, spilled, rows_all,
    core_out, core_in, mine, across_out, across_in, kept, summed, final_out, near_in, far_in,
    count_send, count_recv, w_send, w_recv, spill_send, spill_recv,
    own_send, relay_send, rows_recv, core_send, core_recv, across_send, across_recv,
    near_send, near_recv, far_send, far_recv, load_sem, ids_sem, w_sem, res_sem,
):
    devices = layers * HALVES
    cap = q_ref.shape[0]
    width = q_ref.shape[1]
    half_rows = rows_all.shape[2]
    part_width = width // PARTS
    quarter = kept.shape[2]
    per_class = half_rows // PAIR_CLASSES
    both = HALVES * half_rows
    p = lax.axis_index("pairs")
    t = lax.axis_index("tensor")
    z = p // HALVES
    y = p % HALVES
    x = t // 2
    core = t % 2
    beside = (z * HALVES + 1 - y, t)
    other_core = (p, x * 2 + 1 - core)
    other_chip = (p, (1 - x) * 2 + core)

    barrier = pltpu.get_barrier_semaphore()
    everyone = devices * tensors

    def greet(step, carry):
        number = lax.rem(p * tensors + t + step, everyone)
        pl.semaphore_signal(
            barrier, inc=1, device_id=(number // tensors, number % tensors), device_id_type=MESH
        )
        return carry

    loads = {}
    ids_load = pltpu.make_async_copy(ids_hbm, ids_ref, ids_sem)
    ids_load.start()
    for part in range(PARTS):
        columns = slice(part * part_width, (part + 1) * part_width)
        for which, (src, dst) in enumerate(((q_hbm, q_ref), (k_hbm, k_ref), (v_hbm, v_ref))):
            loads[part, which] = pltpu.make_async_copy(
                src.at[:, columns], dst.at[:, columns], load_sem.at[part, which]
            )
            loads[part, which].start()
    w_load = pltpu.make_async_copy(w_ref, w_full.at[y], w_sem)
    w_load.start()
    res_load = pltpu.make_async_copy(res_hbm, res_ref, res_sem)
    res_load.start()

    lax.fori_loop(1, everyone, greet, 0)
    ids_load.wait()

    ids_row = ids_ref[...].astype(F32)
    live = jnp.sum(jnp.where(ids_row < SLOTS, 1.0, 0.0), axis=1, keepdims=True)
    own_count = jnp.broadcast_to(live, count_own.shape).astype(jnp.int32)
    count_own[...] = own_count
    counts[p] = own_count
    ids_wide = jnp.broadcast_to(ids_row, (cap, cap))
    allowed = ids_wide == ids_wide.T
    pl.semaphore_wait(barrier, everyone - 1)

    def remote(src, dst, sent, got, where_to):
        return pltpu.make_async_remote_copy(
            src_ref=src, dst_ref=dst, send_sem=sent, recv_sem=got,
            device_id=where_to, device_id_type=MESH,
        )

    pending = []
    for step in range(1, devices):
        peer = lax.rem(p + step, devices)
        copy = remote(count_own, counts.at[p], count_send.at[step], count_recv.at[p], (peer, t))
        copy.start()
        pending.append(copy)

    piece_rows = w_ref.shape[0] // WEIGHT_PIECES

    def weight_copy(piece, slot):
        rows = pl.ds(piece * piece_rows, piece_rows)
        return remote(
            w_ref.at[rows], w_full.at[slot, rows], w_send.at[piece], w_recv.at[piece], beside
        )

    def send_weights(first, last):
        for piece in range(first, last):
            copy = weight_copy(piece, y)
            copy.start()
            pending.append(copy)

    def rows_copy(block, part, sent, layer):
        here = rows_all.at[block, part]
        return remote(here, here, sent, rows_recv.at[block, part], (layer * HALVES + y, t))

    spill_from = pl.multiple_of((1 - y) * (cap - SPILL), 16)

    def spill_copy(part):
        return remote(
            attended.at[part, pl.ds(spill_from, SPILL)], spilled.at[part],
            spill_send.at[part], spill_recv.at[part], beside,
        )

    def attend_part(part):
        for which in range(3):
            loads[part, which].wait()
        for pair in range(part_width // (2 * HEAD)):
            lanes = slice(part * part_width + pair * 2 * HEAD, part * part_width + (pair + 1) * 2 * HEAD)
            attended[part, :, pair * 2 * HEAD:(pair + 1) * 2 * HEAD] = attend_pair(
                q_ref[:, lanes], k_ref[:, lanes], v_ref[:, lanes], allowed
            )
        copy = spill_copy(part)
        copy.start()
        pending.append(copy)

    send_weights(0, 1)
    attend_part(0)
    send_weights(1, 2)

    for step in range(1, devices):
        source = lax.rem(p + step, devices)
        remote(count_own, counts.at[source], count_send.at[0], count_recv.at[source], (source, t)).wait_recv()

    def start_of(block):
        total = jnp.zeros((1, cap), jnp.int32)
        for earlier in range(devices):
            total = total + jnp.where(earlier < block, counts[earlier, 0:1, :], 0)
        return total

    live_first = counts[HALVES * z, 0:1, :]
    live_second = counts[HALVES * z + 1, 0:1, :]
    second_at = both - live_second - ((both - live_first - live_second) & 7)
    start_pair = start_of(HALVES * z)
    kind, turn = class_and_turn(lax.broadcasted_iota(jnp.int32, (half_rows, cap), 0), per_class)
    slot = y * half_rows + ((kind - start_pair) & 7) + 8 * turn
    column = lax.broadcasted_iota(jnp.int32, (half_rows, cap), 1)
    row_first = slot
    row_second = slot - second_at
    row_own = jnp.where(y == 0, row_first, row_second)
    row_peer = jnp.where(y == 0, row_second, row_first)
    live_own = jnp.where(y == 0, live_first, live_second)
    live_peer = jnp.where(y == 0, live_second, live_first)
    pick_own = jnp.where((column == row_own) & (column < live_own), 1.0, 0.0).astype(BF16)
    peer_from = y * (cap - SPILL)
    pick_peer = jnp.where((column == row_peer - peer_from) & (column + peer_from < live_peer), 1.0, 0.0)
    pick_peer = pick_peer.astype(BF16)[:, :SPILL]

    def share_part(part):
        spill_copy(part).wait_recv()
        packed = jnp.dot(pick_own, attended[part], preferred_element_type=F32)
        packed = packed + jnp.dot(pick_peer, spilled[part], preferred_element_type=F32)
        rows_all[z, part] = packed.astype(BF16)

        @pl.when(z < layers - 1)
        def _():
            rows_copy(z, part, own_send.at[0, part], z + 1).start()

        @pl.when(z > 0)
        def _():
            rows_copy(z, part, own_send.at[1, part], z - 1).start()

    share_part(0)
    for part in range(1, PARTS):
        attend_part(part)
        share_part(part)
    send_weights(2, WEIGHT_PIECES)

    def order_of(layer):
        return (
            layer,
            jnp.where(layer % 2 == 0, layer + 1, layer - 1),
            jnp.where(layer < 2, 2, 1),
            jnp.where(layer < 2, 3, 0),
        )

    order = order_of(z)
    inner = (z > 0) & (z < layers - 1)

    def take_rows(turn_index, relay):
        block = order[turn_index]
        onward = jnp.where(block < z, z + 1, z - 1)
        for part in range(PARTS):
            copy = rows_copy(block, part, relay_send.at[turn_index, part], onward)
            copy.wait_recv()
            if relay:
                copy.start()

    def take_inner(turn_index):
        @pl.when(inner)
        def _():
            take_rows(turn_index, True)

    def take_outer(turn_index):
        @pl.when(jnp.logical_not(inner))
        def _():
            take_rows(turn_index, False)

    def partial_of(turn_index, side):
        block = order[turn_index]
        total = jnp.zeros((half_rows, w_ref.shape[1]), F32)
        for part in range(PARTS):
            total = total + jnp.dot(
                rows_all[block, part],
                w_full[side, part * part_width:(part + 1) * part_width, :],
                preferred_element_type=F32,
            )
        return total

    def core_copy(turn_index):
        return remote(
            core_out.at[turn_index], core_in.at[turn_index],
            core_send.at[turn_index], core_recv.at[turn_index], other_core,
        )

    def across_copy(turn_index):
        return remote(
            across_out.at[turn_index], across_in.at[turn_index],
            across_send.at[turn_index], across_recv.at[turn_index], other_chip,
        )

    def multiply(turn_index, side):
        value = partial_of(turn_index, side).astype(BF16)

        @pl.when(core == side)
        def _():
            mine[turn_index] = value

        @pl.when(core != side)
        def _():
            core_out[turn_index] = value
            core_copy(turn_index).start()

    def add_cores(turn_index):
        core_copy(turn_index).wait_recv()
        total = mine[turn_index].astype(F32) + core_in[turn_index].astype(F32)
        left, right = total[:, :quarter], total[:, quarter:]
        across_out[turn_index] = jnp.where(x == 0, right, left).astype(BF16)
        kept[turn_index] = jnp.where(x == 0, left, right)
        across_copy(turn_index).start()

    def add_chips(turn_index):
        across_copy(turn_index).wait_recv()
        total = kept[turn_index] + across_in[turn_index].astype(F32)
        summed[:, turn_index] = total.reshape(PAIR_CLASSES, per_class, quarter)

    batch_turns = layers // BATCHES
    batch_rows = batch_turns * per_class
    my_source = y * 2 + core
    kind = jnp.where(x == z // 2, 0, 1)
    lands_here = core == z % 2

    def near_copy(batch, step):
        peer = lax.rem(p + step, devices)
        return remote(
            final_out.at[batch, peer], near_in.at[kind, batch, my_source],
            near_send.at[batch, step], near_recv.at[kind, batch, my_source],
            (peer, x * 2 + z % 2),
        )

    def far_copy(batch, source):
        return remote(
            near_in.at[1, batch, source], far_in.at[batch, source],
            far_send.at[batch, source], far_recv.at[batch, source], other_chip,
        )

    def wait_near(which, batch, source):
        sender_layer = jnp.where(which == 0, x, 1 - x) * 2 + core
        from_self = (z == sender_layer) & (my_source == source)

        @pl.when(jnp.logical_not(from_self))
        def _():
            remote(
                final_out.at[0, 0], near_in.at[which, batch, source], near_send.at[0, 0],
                near_recv.at[which, batch, source], other_chip,
            ).wait_recv()

    def spread(batch):
        turns = slice(batch * batch_turns, (batch + 1) * batch_turns)
        for turn_index in range(layers)[turns]:
            add_chips(turn_index)
        final_out[batch] = summed[:, turns].reshape(devices, batch_rows, quarter).astype(BF16)
        for step in range(1, devices):
            near_copy(batch, step).start()

        @pl.when(lands_here)
        def _():
            near_in[kind, batch, my_source] = final_out[batch, p]

        @pl.when(jnp.logical_not(lands_here))
        def _():
            near_copy(batch, 0).start()

    def pass_on(batch):
        for source in range(2 * HALVES):
            wait_near(1, batch, source)
            far_copy(batch, source).start()

    last = layers - 1
    w_load.wait()
    multiply(0, y)
    for turn_index in range(1, last):
        take_inner(turn_index)
        take_outer(turn_index)
        multiply(turn_index, y)

        @pl.when(core == y)
        def _():
            add_cores(turn_index - 1)

    take_inner(last)

    @pl.when(core == y)
    def _():
        add_cores(last - 1)
        spread(0)

    for piece in range(WEIGHT_PIECES):
        weight_copy(piece, 1 - y).wait_recv()

    for turn_index in range(last):
        multiply(turn_index, 1 - y)

        @pl.when(core != y)
        def _():
            add_cores(turn_index)

    @pl.when(core != y)
    def _():
        spread(0)

    take_outer(last)
    core_out[last] = partial_of(last, 1 - core).astype(BF16)
    core_copy(last).start()
    mine[last] = partial_of(last, core).astype(BF16)
    add_cores(last)
    pass_on(0)
    for batch in range(1, BATCHES):
        spread(batch)

    place_shape = (half_rows, HALVES * layers * per_class)
    lane = lax.broadcasted_iota(jnp.int32, (1, place_shape[1]), 1)
    side = jnp.where(lane >= layers * per_class, 1, 0)
    lane = lane - side * layers * per_class
    layer = jnp.zeros_like(lane)
    for bound in range(1, layers):
        layer = layer + jnp.where(lane >= bound * per_class, 1, 0)
    lane = lane - layer * per_class
    spot = jnp.zeros_like(lane) - 1
    count_width = place_shape[1]
    sender_order = order_of(t)
    for turn_index in range(layers):
        block = sender_order[turn_index]
        first = counts[HALVES * block, 0:1, :][:, :count_width]
        second = counts[HALVES * block + 1, 0:1, :][:, :count_width]
        begin = start_of(HALVES * block)[:, :count_width]
        second_from = both - second - ((both - first - second) & 7)
        where_at = side * half_rows + ((p - begin) & 7) + 8 * lane
        number = jnp.where(
            where_at < first, begin + where_at,
            jnp.where(
                (where_at >= second_from) & (where_at < second_from + second),
                begin + first + where_at - second_from, -8,
            ),
        )
        spot = jnp.where(layer == turn_index, number >> 3, spot)
    place = jnp.where(
        lax.broadcasted_iota(jnp.int32, place_shape, 0) == spot, 1.0, 0.0
    ).astype(BF16)

    for batch in range(1, BATCHES):
        pass_on(batch)
    res_load.wait()

    def place_rows(source_core, source_x, ref):
        columns = pl.ds(pl.multiple_of((source_core * 2 + source_x) * quarter, quarter), quarter)
        rows = jnp.concatenate(
            [ref[batch, half * 2 + source_core] for half in range(HALVES) for batch in range(BATCHES)],
            axis=0,
        )
        moved = jnp.dot(place, rows, preferred_element_type=F32)
        out_ref[:, columns] = (res_ref[:, columns].astype(F32) + moved).astype(BF16)

    for batch in range(BATCHES):
        for source in range(2 * HALVES):
            wait_near(0, batch, source)
    for source_core in range(2):
        place_rows(source_core, x, near_in.at[0])
    for batch in range(BATCHES):
        for source in range(2 * HALVES):
            far_copy(batch, source).wait_recv()
    for source_core in range(2):
        place_rows(source_core, 1 - x, far_in)

    for copy in pending:
        copy.wait_send()
    for turn_index in range(layers):
        core_copy(turn_index).wait_send()
        across_copy(turn_index).wait_send()
    for part in range(PARTS):
        @pl.when(z < layers - 1)
        def _():
            rows_copy(z, part, own_send.at[0, part], z + 1).wait_send()

        @pl.when(z > 0)
        def _():
            rows_copy(z, part, own_send.at[1, part], z - 1).wait_send()

    @pl.when(inner)
    def _():
        for turn_index in range(1, layers):
            block = order[turn_index]
            onward = jnp.where(block < z, z + 1, z - 1)
            for part in range(PARTS):
                rows_copy(block, part, relay_send.at[turn_index, part], onward).wait_send()

    for batch in range(BATCHES):
        for step in range(1, devices):
            near_copy(batch, step).wait_send()
        for source in range(2 * HALVES):
            far_copy(batch, source).wait_send()

        @pl.when(jnp.logical_not(lands_here))
        def _():
            near_copy(batch, 0).wait_send()


def fused_shards(layers, tensors, queries, key_rows, value_rows, pair_ids, out_weight, residual):
    devices = layers * HALVES
    cap, width = queries.shape
    half_rows = residual.shape[0]
    columns = out_weight.shape[1]
    quarter = columns // 2
    part_width = width // PARTS
    per_class = half_rows // PAIR_CLASSES
    batch_rows = layers // BATCHES * per_class
    dma = pltpu.SemaphoreType.DMA
    vmem = pltpu.VMEM
    scratch = [
        vmem((cap, width), BF16), vmem((cap, width), BF16), vmem((cap, width), BF16),
        vmem((1, cap), jnp.int32),
        vmem(residual.shape, BF16),
        vmem((8, cap), jnp.int32),
        vmem((devices, 8, cap), jnp.int32),
        vmem((HALVES, width, columns), BF16),
        vmem((PARTS, cap, part_width), BF16),
        vmem((PARTS, SPILL, part_width), BF16),
        vmem((layers, PARTS, half_rows, part_width), BF16),
        vmem((layers, half_rows, columns), BF16),
        vmem((layers, half_rows, columns), BF16),
        vmem((layers, half_rows, columns), BF16),
        vmem((layers, half_rows, quarter), BF16),
        vmem((layers, half_rows, quarter), BF16),
        vmem((layers, half_rows, quarter), F32),
        vmem((PAIR_CLASSES, layers, per_class, quarter), F32),
        vmem((BATCHES, devices, batch_rows, quarter), BF16),
        vmem((2, BATCHES, 2 * HALVES, batch_rows, quarter), BF16),
        vmem((BATCHES, 2 * HALVES, batch_rows, quarter), BF16),
        dma((devices,)), dma((devices,)),
        dma((WEIGHT_PIECES,)), dma((WEIGHT_PIECES,)),
        dma((PARTS,)), dma((PARTS,)),
        dma((2, PARTS)), dma((layers, PARTS)), dma((layers, PARTS)),
        dma((layers,)), dma((layers,)),
        dma((layers,)), dma((layers,)),
        dma((BATCHES, devices)), dma((2, BATCHES, 2 * HALVES)),
        dma((BATCHES, 2 * HALVES)), dma((BATCHES, 2 * HALVES)),
        dma((PARTS, 3)), dma, dma, dma,
    ]
    in_vmem = pl.BlockSpec(memory_space=pltpu.VMEM)
    return pl.pallas_call(
        functools.partial(fused_kernel, layers, tensors),
        out_shape=jax.ShapeDtypeStruct(residual.shape, residual.dtype),
        in_specs=[pl.BlockSpec(memory_space=pltpu.HBM)] * 6,
        out_specs=in_vmem,
        scratch_shapes=scratch,
        compiler_params=pltpu.CompilerParams(
            collective_id=0, has_side_effects=True, vmem_limit_bytes=56 * 1024 * 1024
        ),
    )(queries, key_rows, value_rows, pair_ids.reshape(1, cap), out_weight, residual)


def fits_fused(mesh):
    layers = mesh.shape["pairs"] // HALVES
    return mesh.shape["tensor"] == 4 and layers == 4


def solution(mesh):
    in_specs = (
        P("pairs", "tensor"),
        P("pairs", "tensor"),
        P("pairs", "tensor"),
        P("pairs"),
        P("tensor", "pairs"),
        P("pairs", "tensor"),
    )
    out_specs = P("pairs", "tensor")
    per_device = shards
    if fits_fused(mesh):
        per_device = functools.partial(fused_shards, mesh.shape["pairs"] // HALVES, mesh.shape["tensor"])
    return jax.shard_map(per_device, mesh=mesh, in_specs=in_specs, out_specs=out_specs, check_vma=False)
```

```python
import functools

import jax
import jax.numpy as jnp
from jax import lax
from jax.experimental import pallas as pl
from jax.experimental.pallas import tpu as pltpu
from jax.sharding import PartitionSpec as P

HEAD = 64
SLOTS = 8


def carried_in(part, axis, combine, identity):
    place = lax.axis_index(axis)
    gathered = lax.all_gather(part, axis)
    state = jnp.zeros_like(part) + jnp.asarray(identity, part.dtype)

    def one(step, state):
        return combine(state, lax.dynamic_index_in_dim(gathered, step, 0, False))

    return lax.fori_loop(0, place, one, state)


def attend_group(query_part, key_part, value_part, allowed):
    scores = jnp.einsum("qhd,khd->hqk", query_part, key_part, preferred_element_type=jnp.float32)
    masked = jnp.where(allowed[None], scores, -1e30)
    row_top = jnp.max(masked, axis=2, keepdims=True)
    exp_terms = jnp.where(allowed[None], jnp.exp(masked - row_top), 0.0)
    row_total = jnp.maximum(jnp.sum(exp_terms, axis=2, keepdims=True), 1.0)
    weights = (exp_terms / row_total).astype(jnp.bfloat16)
    mixed = jnp.einsum("hqk,khd->qhd", weights, value_part, preferred_element_type=jnp.float32)
    return mixed.astype(jnp.bfloat16)


def add_counts(earlier, later):
    return earlier + later


def shards(queries, key_rows, value_rows, pair_ids, out_weight, residual):
    cap_rows = queries.shape[0]
    local_width = queries.shape[1]
    heads_local = local_width // HEAD
    group_size = 4
    balanced_rows = residual.shape[0]
    allowed = (pair_ids[:, None] == pair_ids[None, :]) & (pair_ids[:, None] < SLOTS)

    def split_heads(stacked):
        return stacked.reshape(cap_rows, heads_local // group_size, group_size, HEAD).transpose(
            1, 0, 2, 3
        )

    def per_group(operands):
        return attend_group(operands[0], operands[1], operands[2], allowed)

    grouped = lax.map(
        per_group, (split_heads(queries), split_heads(key_rows), split_heads(value_rows))
    )
    attended = grouped.transpose(1, 0, 2, 3).reshape(cap_rows, local_width)
    live_rows = jnp.sum((pair_ids < SLOTS).astype(jnp.int32))
    devices = lax.axis_size("pairs")
    row_start = carried_in(live_rows.reshape(1), "pairs", add_counts, jnp.zeros((1,), jnp.int32))[0]
    partial_value = jnp.dot(
        attended,
        lax.all_gather(out_weight, "pairs", axis=1, tiled=True),
        preferred_element_type=jnp.float32,
    )
    payload = lax.psum_scatter(
        partial_value.astype(jnp.bfloat16), "tensor", scatter_dimension=1, tiled=True
    )
    per_peer = cap_rows // devices
    feature_width = payload.shape[1]
    peer_index = jnp.arange(devices, dtype=jnp.int32)
    turn_index = jnp.arange(per_peer, dtype=jnp.int32)
    source_rows = ((peer_index - row_start) % devices)[:, None] + devices * turn_index[None, :]
    slot_index = jnp.where(
        source_rows < live_rows, (row_start + source_rows) // devices, balanced_rows
    ).astype(jnp.int32)
    outgoing = jnp.take(payload, source_rows.reshape(-1), axis=0).reshape(
        devices, per_peer, feature_width
    )
    incoming = lax.all_to_all(outgoing, "pairs", split_axis=0, concat_axis=0, tiled=True)
    incoming_slots = lax.all_to_all(slot_index, "pairs", split_axis=0, concat_axis=0, tiled=True)
    landed = jnp.zeros((balanced_rows, feature_width), payload.dtype)
    moved_rows = landed.at[incoming_slots.reshape(-1)].set(
        incoming.reshape(-1, feature_width), mode="drop"
    )
    return (residual.astype(jnp.float32) + moved_rows.astype(jnp.float32)).astype(jnp.bfloat16)


HALVES = 2
PARTS = 4
WEIGHT_PIECES = 8
SPILL = 80
PAIR_CLASSES = 8
MESH = pl.DeviceIdType.MESH
BF16 = jnp.bfloat16
F32 = jnp.float32


def attend_pair(query_pair, key_pair, value_pair, bias):
    low = lax.broadcasted_iota(jnp.int32, query_pair.shape, 1) < HEAD
    zero = jnp.zeros_like(query_pair)
    one = jnp.ones_like(value_pair)
    queries = (jnp.where(low, query_pair, zero), jnp.where(low, zero, query_pair))
    values = (jnp.where(low, value_pair, one), jnp.where(low, one, value_pair))
    mixed = []
    for query_one, value_one in zip(queries, values):
        scores = lax.dot_general(
            query_one, key_pair, (((1,), (1,)), ((), ())), preferred_element_type=F32
        )
        masked = scores + bias
        exp_terms = jnp.exp(masked - jnp.max(masked, axis=1, keepdims=True)).astype(BF16)
        mixed.append(jnp.dot(exp_terms, value_one, preferred_element_type=F32))
    sums = jnp.where(low, mixed[0], mixed[1])
    totals = pltpu.roll(jnp.where(low, mixed[1], mixed[0]), HEAD, 1)
    return (sums / totals).astype(BF16)


def class_and_turn(place, per_class):
    kind = jnp.zeros_like(place)
    for bound in range(1, PAIR_CLASSES):
        kind = kind + jnp.where(place >= bound * per_class, 1, 0)
    return kind, place - per_class * kind


def fused_kernel(
    layers, tensors,
    q_hbm, k_hbm, v_hbm, ids_hbm, w_ref, res_hbm, out_ref,
    q_ref, k_ref, v_ref, ids_ref, res_ref,
    bias, acc, count_own, counts, w_full, attended, spilled, rows_all,
    core_out, core_in, mine, across_out, across_in, kept, summed, final_out, final_in,
    count_send, count_recv, w_send, w_recv, spill_send, spill_recv,
    own_send, relay_send, rows_recv, core_send, core_recv, across_send, across_recv,
    final_send, final_recv, load_sem, ids_sem, w_sem, res_sem,
):
    devices = layers * HALVES
    cap = q_ref.shape[0]
    width = q_ref.shape[1]
    half_rows = rows_all.shape[1]
    part_width = width // PARTS
    quarter = final_in.shape[2]
    per_class = half_rows // PAIR_CLASSES
    both = HALVES * half_rows
    p = lax.axis_index("pairs")
    t = lax.axis_index("tensor")
    z = p // HALVES
    y = p % HALVES
    x = t // 2
    core = t % 2
    beside = (z * HALVES + 1 - y, t)
    other_core = (p, x * 2 + 1 - core)
    other_chip = (p, (1 - x) * 2 + core)

    barrier = pltpu.get_barrier_semaphore()
    everyone = devices * tensors

    def greet(step, carry):
        number = lax.rem(p * tensors + t + step, everyone)
        pl.semaphore_signal(
            barrier, inc=1, device_id=(number // tensors, number % tensors), device_id_type=MESH
        )
        return carry

    loads = {}
    ids_load = pltpu.make_async_copy(ids_hbm, ids_ref, ids_sem)
    ids_load.start()
    for part in range(PARTS):
        columns = slice(part * part_width, (part + 1) * part_width)
        for which, (src, dst) in enumerate(((q_hbm, q_ref), (k_hbm, k_ref), (v_hbm, v_ref))):
            loads[part, which] = pltpu.make_async_copy(
                src.at[:, columns], dst.at[:, columns], load_sem.at[part, which]
            )
            loads[part, which].start()
    w_load = pltpu.make_async_copy(w_ref, w_full.at[y], w_sem)
    w_load.start()
    res_load = pltpu.make_async_copy(res_hbm, res_ref, res_sem)
    res_load.start()

    lax.fori_loop(1, everyone, greet, 0)
    ids_load.wait()

    ids_row = ids_ref[...].astype(F32)
    live = jnp.sum(jnp.where(ids_row < SLOTS, 1.0, 0.0), axis=1, keepdims=True)
    own_count = jnp.broadcast_to(live, count_own.shape).astype(jnp.int32)
    count_own[...] = own_count
    counts[p] = own_count
    ids_wide = jnp.broadcast_to(ids_row, (cap, cap))
    bias[...] = jnp.where(ids_wide == ids_wide.T, 0.0, -1e30)
    pl.semaphore_wait(barrier, everyone - 1)

    def remote(src, dst, sent, got, where_to):
        return pltpu.make_async_remote_copy(
            src_ref=src, dst_ref=dst, send_sem=sent, recv_sem=got,
            device_id=where_to, device_id_type=MESH,
        )

    pending = []
    for step in range(1, devices):
        peer = lax.rem(p + step, devices)
        copy = remote(count_own, counts.at[p], count_send.at[step], count_recv.at[p], (peer, t))
        copy.start()
        pending.append(copy)

    piece_rows = w_ref.shape[0] // WEIGHT_PIECES

    def weight_copy(piece, slot):
        rows = pl.ds(piece * piece_rows, piece_rows)
        return remote(
            w_ref.at[rows], w_full.at[slot, rows], w_send.at[piece], w_recv.at[piece], beside
        )

    def send_weights(first, last):
        for piece in range(first, last):
            copy = weight_copy(piece, y)
            copy.start()
            pending.append(copy)

    def rows_copy(block, part, sent, layer):
        here = rows_all.at[block, :, pl.ds(part * part_width, part_width)]
        return remote(here, here, sent, rows_recv.at[block, part], (layer * HALVES + y, t))

    spill_from = pl.multiple_of((1 - y) * (cap - SPILL), 16)

    def spill_copy(part):
        return remote(
            attended.at[pl.ds(spill_from, SPILL), pl.ds(part * part_width, part_width)], spilled.at[part],
            spill_send.at[part], spill_recv.at[part], beside,
        )

    def attend_part(part):
        for which in range(3):
            loads[part, which].wait()
        for pair in range(part_width // (2 * HEAD)):
            lanes = slice(part * part_width + pair * 2 * HEAD, part * part_width + (pair + 1) * 2 * HEAD)
            attended[:, lanes] = attend_pair(
                q_ref[:, lanes], k_ref[:, lanes], v_ref[:, lanes], bias[...]
            )
        copy = spill_copy(part)
        copy.start()
        pending.append(copy)

    send_weights(0, 2)
    attend_part(0)
    send_weights(2, 3)

    for step in range(1, devices):
        source = lax.rem(p + step, devices)
        remote(count_own, counts.at[source], count_send.at[0], count_recv.at[source], (source, t)).wait_recv()

    def start_of(block):
        total = jnp.zeros((1, cap), jnp.int32)
        for earlier in range(devices):
            total = total + jnp.where(earlier < block, counts[earlier, 0:1, :], 0)
        return total

    live_first = counts[HALVES * z, 0:1, :]
    live_second = counts[HALVES * z + 1, 0:1, :]
    second_at = both - live_second - ((both - live_first - live_second) & 7)
    start_pair = start_of(HALVES * z)
    kind, turn = class_and_turn(lax.broadcasted_iota(jnp.int32, (half_rows, cap), 0), per_class)
    slot = y * half_rows + ((kind - start_pair) & 7) + 8 * turn
    column = lax.broadcasted_iota(jnp.int32, (half_rows, cap), 1)
    row_first = slot
    row_second = slot - second_at
    row_own = jnp.where(y == 0, row_first, row_second)
    row_peer = jnp.where(y == 0, row_second, row_first)
    live_own = jnp.where(y == 0, live_first, live_second)
    live_peer = jnp.where(y == 0, live_second, live_first)
    pick_own = jnp.where((column == row_own) & (column < live_own), 1.0, 0.0).astype(BF16)
    peer_from = y * (cap - SPILL)
    pick_peer = jnp.where((column == row_peer - peer_from) & (column + peer_from < live_peer), 1.0, 0.0)
    pick_peer = pick_peer.astype(BF16)[:, :SPILL]

    def share_part(part):
        spill_copy(part).wait_recv()
        columns = slice(part * part_width, (part + 1) * part_width)
        packed = jnp.dot(pick_own, attended[:, columns], preferred_element_type=F32)
        packed = packed + jnp.dot(pick_peer, spilled[part], preferred_element_type=F32)
        rows_all[z, :, columns] = packed.astype(BF16)

        @pl.when(z < layers - 1)
        def _():
            rows_copy(z, part, own_send.at[0, part], z + 1).start()

        @pl.when(z > 0)
        def _():
            rows_copy(z, part, own_send.at[1, part], z - 1).start()

    share_part(0)
    for part in range(1, PARTS):
        attend_part(part)
        if part < PARTS - 1:
            send_weights(2 + part, 3 + part)
        share_part(part)
    send_weights(1 + PARTS, WEIGHT_PIECES)

    order = (
        z,
        jnp.where(z % 2 == 0, z + 1, z - 1),
        jnp.where(z < 2, 2, 1),
        jnp.where(z < 2, 3, 0),
    )
    inner = (z > 0) & (z < layers - 1)

    def take_rows(turn_index, relay):
        block = order[turn_index]
        onward = jnp.where(block < z, z + 1, z - 1)
        for part in range(PARTS):
            copy = rows_copy(block, part, relay_send.at[turn_index, part], onward)
            copy.wait_recv()
            if relay:
                copy.start()

    def take_inner(turn_index):
        @pl.when(inner)
        def _():
            take_rows(turn_index, True)

    def take_outer(turn_index):
        @pl.when(jnp.logical_not(inner))
        def _():
            take_rows(turn_index, False)

    def partial_of(turn_index, side, first=0, end=width):
        return jnp.dot(
            rows_all[order[turn_index], :, first:end], w_full[side, first:end, :],
            preferred_element_type=F32,
        )

    def core_copy(turn_index):
        return remote(
            core_out.at[turn_index], core_in.at[turn_index],
            core_send.at[turn_index], core_recv.at[turn_index], other_core,
        )

    def across_copy(turn_index):
        return remote(
            across_out.at[turn_index], across_in.at[turn_index],
            across_send.at[turn_index], across_recv.at[turn_index], other_chip,
        )

    def multiply(turn_index, side):
        hand_out(turn_index, side, partial_of(turn_index, side))

    def hand_out(turn_index, side, total):
        value = total.astype(BF16)

        @pl.when(core == side)
        def _():
            mine[turn_index] = value

        @pl.when(core != side)
        def _():
            core_out[turn_index] = value
            core_copy(turn_index).start()

    def add_cores(turn_index):
        core_copy(turn_index).wait_recv()
        total = mine[turn_index].astype(F32) + core_in[turn_index].astype(F32)
        left, right = total[:, :quarter], total[:, quarter:]
        across_out[turn_index] = jnp.where(x == 0, right, left).astype(BF16)
        kept[turn_index] = jnp.where(x == 0, left, right)
        across_copy(turn_index).start()

    def add_chips(turn_index):
        across_copy(turn_index).wait_recv()
        total = kept[turn_index] + across_in[turn_index].astype(F32)
        summed[:, order[turn_index]] = total.reshape(PAIR_CLASSES, per_class, quarter)

    last = layers - 1
    w_load.wait()
    multiply(0, y)
    for turn_index in range(1, last):
        take_inner(turn_index)
        take_outer(turn_index)
        multiply(turn_index, y)

        @pl.when(core == y)
        def _():
            add_cores(turn_index - 1)

    take_inner(last)

    @pl.when(core == y)
    def _():
        add_cores(last - 1)

    half_pieces = WEIGHT_PIECES // 2
    half_depth = width // 2
    for piece in range(half_pieces):
        weight_copy(piece, 1 - y).wait_recv()
    for turn_index in range(last):
        acc[turn_index] = partial_of(turn_index, 1 - y, 0, half_depth)
    for piece in range(half_pieces, WEIGHT_PIECES):
        weight_copy(piece, 1 - y).wait_recv()

    for turn_index in range(last):
        hand_out(
            turn_index, 1 - y,
            acc[turn_index] + partial_of(turn_index, 1 - y, half_depth, width),
        )

        @pl.when(core != y)
        def _():
            add_cores(turn_index)

    take_outer(last)
    core_out[last] = partial_of(last, 1 - core).astype(BF16)
    core_copy(last).start()
    mine[last] = partial_of(last, core).astype(BF16)
    add_cores(last)
    for turn_index in range(layers):
        add_chips(turn_index)

    final_out[...] = summed[...].reshape(final_out.shape).astype(BF16)
    source_slot = y * tensors + core * 2 + x
    to_self = z == t

    def final_copy(step):
        peer = lax.rem(p + step, devices)
        return remote(
            final_out.at[peer], final_in.at[source_slot],
            final_send.at[step], final_recv.at[source_slot], (peer, z),
        )

    for step in range(1, devices):
        copy = final_copy(step)
        copy.start()
        pending.append(copy)

    @pl.when(to_self)
    def _():
        final_in[source_slot] = final_out[p]

    @pl.when(jnp.logical_not(to_self))
    def _():
        final_copy(0).start()

    place_shape = (half_rows, HALVES * layers * per_class)
    lane = lax.broadcasted_iota(jnp.int32, (1, place_shape[1]), 1)
    side = jnp.where(lane >= layers * per_class, 1, 0)
    lane = lane - side * layers * per_class
    layer = jnp.zeros_like(lane)
    for bound in range(1, layers):
        layer = layer + jnp.where(lane >= bound * per_class, 1, 0)
    lane = lane - layer * per_class
    spot = jnp.zeros_like(lane) - 1
    count_width = place_shape[1]
    for block in range(layers):
        first = counts[HALVES * block, 0:1, :][:, :count_width]
        second = counts[HALVES * block + 1, 0:1, :][:, :count_width]
        begin = start_of(HALVES * block)[:, :count_width]
        second_from = both - second - ((both - first - second) & 7)
        where_at = side * half_rows + ((p - begin) & 7) + 8 * lane
        number = jnp.where(
            where_at < first, begin + where_at,
            jnp.where(
                (where_at >= second_from) & (where_at < second_from + second),
                begin + first + where_at - second_from, -8,
            ),
        )
        spot = jnp.where(layer == block, number >> 3, spot)
    place = jnp.where(
        lax.broadcasted_iota(jnp.int32, place_shape, 0) == spot, 1.0, 0.0
    ).astype(BF16)

    for half in range(HALVES):
        for piece in range(tensors):
            slot_index = half * tensors + piece
            from_self = (z == t) & (source_slot == slot_index)

            @pl.when(jnp.logical_not(from_self))
            def _():
                remote(
                    final_out.at[0], final_in.at[slot_index], final_send.at[0],
                    final_recv.at[slot_index], (lax.rem(p + 1, devices), t),
                ).wait_recv()

    res_load.wait()
    depth = layers * per_class
    for piece in range(tensors):
        columns = slice(piece * quarter, (piece + 1) * quarter)
        moved = res_ref[:, columns].astype(F32)
        for half in range(HALVES):
            moved = moved + jnp.dot(
                place[:, half * depth:(half + 1) * depth],
                final_in[half * tensors + piece], preferred_element_type=F32,
            )
        out_ref[:, columns] = moved.astype(BF16)

    for copy in pending:
        copy.wait_send()
    for turn_index in range(layers):
        core_copy(turn_index).wait_send()
        across_copy(turn_index).wait_send()
    for part in range(PARTS):
        @pl.when(z < layers - 1)
        def _():
            rows_copy(z, part, own_send.at[0, part], z + 1).wait_send()

        @pl.when(z > 0)
        def _():
            rows_copy(z, part, own_send.at[1, part], z - 1).wait_send()

    @pl.when(inner)
    def _():
        for turn_index in range(1, layers):
            block = order[turn_index]
            onward = jnp.where(block < z, z + 1, z - 1)
            for part in range(PARTS):
                rows_copy(block, part, relay_send.at[turn_index, part], onward).wait_send()

    @pl.when(jnp.logical_not(to_self))
    def _():
        final_copy(0).wait_send()


def fused_shards(layers, tensors, queries, key_rows, value_rows, pair_ids, out_weight, residual):
    devices = layers * HALVES
    cap, width = queries.shape
    half_rows = residual.shape[0]
    columns = out_weight.shape[1]
    quarter = columns // 2
    part_width = width // PARTS
    per_class = half_rows // PAIR_CLASSES
    depth = layers * per_class
    dma = pltpu.SemaphoreType.DMA
    vmem = pltpu.VMEM
    scratch = [
        vmem((cap, width), BF16), vmem((cap, width), BF16), vmem((cap, width), BF16),
        vmem((1, cap), jnp.int32),
        vmem(residual.shape, BF16),
        vmem((cap, cap), F32),
        vmem((layers - 1, half_rows, columns), F32),
        vmem((8, cap), jnp.int32),
        vmem((devices, 8, cap), jnp.int32),
        vmem((HALVES, width, columns), BF16),
        vmem((cap, width), BF16),
        vmem((PARTS, SPILL, part_width), BF16),
        vmem((layers, half_rows, width), BF16),
        vmem((layers, half_rows, columns), BF16),
        vmem((layers, half_rows, columns), BF16),
        vmem((layers, half_rows, columns), BF16),
        vmem((layers, half_rows, quarter), BF16),
        vmem((layers, half_rows, quarter), BF16),
        vmem((layers, half_rows, quarter), F32),
        vmem((PAIR_CLASSES, layers, per_class, quarter), F32),
        vmem((devices, depth, quarter), BF16),
        vmem((HALVES * tensors, depth, quarter), BF16),
        dma((devices,)), dma((devices,)),
        dma((WEIGHT_PIECES,)), dma((WEIGHT_PIECES,)),
        dma((PARTS,)), dma((PARTS,)),
        dma((2, PARTS)), dma((layers, PARTS)), dma((layers, PARTS)),
        dma((layers,)), dma((layers,)),
        dma((layers,)), dma((layers,)),
        dma((devices,)), dma((HALVES * tensors,)),
        dma((PARTS, 3)), dma, dma, dma,
    ]
    in_vmem = pl.BlockSpec(memory_space=pltpu.VMEM)
    return pl.pallas_call(
        functools.partial(fused_kernel, layers, tensors),
        out_shape=jax.ShapeDtypeStruct(residual.shape, residual.dtype),
        in_specs=[pl.BlockSpec(memory_space=pl.ANY)] * 6,
        out_specs=in_vmem,
        scratch_shapes=scratch,
        compiler_params=pltpu.CompilerParams(
            collective_id=0, has_side_effects=True, vmem_limit_bytes=56 * 1024 * 1024
        ),
    )(queries, key_rows, value_rows, pair_ids.reshape(1, cap), out_weight, residual)


def fits_fused(mesh):
    layers = mesh.shape["pairs"] // HALVES
    return mesh.shape["tensor"] == 4 and layers == 4


def solution(mesh):
    in_specs = (
        P("pairs", "tensor"),
        P("pairs", "tensor"),
        P("pairs", "tensor"),
        P("pairs"),
        P("tensor", "pairs"),
        P("pairs", "tensor"),
    )
    out_specs = P("pairs", "tensor")
    per_device = shards
    if fits_fused(mesh):
        per_device = functools.partial(fused_shards, mesh.shape["pairs"] // HALVES, mesh.shape["tensor"])
    return jax.shard_map(per_device, mesh=mesh, in_specs=in_specs, out_specs=out_specs, check_vma=False)
```

```python
import functools

import jax
import jax.numpy as jnp
from jax import lax
from jax.experimental import pallas as pl
from jax.experimental.pallas import tpu as pltpu
from jax.sharding import PartitionSpec as P

HEAD = 64
SLOTS = 8


def carried_in(part, axis, combine, identity):
    place = lax.axis_index(axis)
    gathered = lax.all_gather(part, axis)
    state = jnp.zeros_like(part) + jnp.asarray(identity, part.dtype)

    def one(step, state):
        return combine(state, lax.dynamic_index_in_dim(gathered, step, 0, False))

    return lax.fori_loop(0, place, one, state)


def attend_group(query_part, key_part, value_part, allowed):
    scores = jnp.einsum("qhd,khd->hqk", query_part, key_part, preferred_element_type=jnp.float32)
    masked = jnp.where(allowed[None], scores, -1e30)
    row_top = jnp.max(masked, axis=2, keepdims=True)
    exp_terms = jnp.where(allowed[None], jnp.exp(masked - row_top), 0.0)
    row_total = jnp.maximum(jnp.sum(exp_terms, axis=2, keepdims=True), 1.0)
    weights = (exp_terms / row_total).astype(jnp.bfloat16)
    mixed = jnp.einsum("hqk,khd->qhd", weights, value_part, preferred_element_type=jnp.float32)
    return mixed.astype(jnp.bfloat16)


def add_counts(earlier, later):
    return earlier + later


def shards(queries, key_rows, value_rows, pair_ids, out_weight, residual):
    cap_rows = queries.shape[0]
    local_width = queries.shape[1]
    heads_local = local_width // HEAD
    group_size = 4
    balanced_rows = residual.shape[0]
    allowed = (pair_ids[:, None] == pair_ids[None, :]) & (pair_ids[:, None] < SLOTS)

    def split_heads(stacked):
        return stacked.reshape(cap_rows, heads_local // group_size, group_size, HEAD).transpose(
            1, 0, 2, 3
        )

    def per_group(operands):
        return attend_group(operands[0], operands[1], operands[2], allowed)

    grouped = lax.map(
        per_group, (split_heads(queries), split_heads(key_rows), split_heads(value_rows))
    )
    attended = grouped.transpose(1, 0, 2, 3).reshape(cap_rows, local_width)
    live_rows = jnp.sum((pair_ids < SLOTS).astype(jnp.int32))
    devices = lax.axis_size("pairs")
    row_start = carried_in(live_rows.reshape(1), "pairs", add_counts, jnp.zeros((1,), jnp.int32))[0]
    partial_value = jnp.dot(
        attended,
        lax.all_gather(out_weight, "pairs", axis=1, tiled=True),
        preferred_element_type=jnp.float32,
    )
    payload = lax.psum_scatter(
        partial_value.astype(jnp.bfloat16), "tensor", scatter_dimension=1, tiled=True
    )
    per_peer = cap_rows // devices
    feature_width = payload.shape[1]
    peer_index = jnp.arange(devices, dtype=jnp.int32)
    turn_index = jnp.arange(per_peer, dtype=jnp.int32)
    source_rows = ((peer_index - row_start) % devices)[:, None] + devices * turn_index[None, :]
    slot_index = jnp.where(
        source_rows < live_rows, (row_start + source_rows) // devices, balanced_rows
    ).astype(jnp.int32)
    outgoing = jnp.take(payload, source_rows.reshape(-1), axis=0).reshape(
        devices, per_peer, feature_width
    )
    incoming = lax.all_to_all(outgoing, "pairs", split_axis=0, concat_axis=0, tiled=True)
    incoming_slots = lax.all_to_all(slot_index, "pairs", split_axis=0, concat_axis=0, tiled=True)
    landed = jnp.zeros((balanced_rows, feature_width), payload.dtype)
    moved_rows = landed.at[incoming_slots.reshape(-1)].set(
        incoming.reshape(-1, feature_width), mode="drop"
    )
    return (residual.astype(jnp.float32) + moved_rows.astype(jnp.float32)).astype(jnp.bfloat16)


HALVES = 2
PARTS = 4
WEIGHT_PIECES = 8
SPILL = 80
PAIR_CLASSES = 8
MESH = pl.DeviceIdType.MESH
BF16 = jnp.bfloat16
F32 = jnp.float32


def attend_pair(query_pair, key_pair, value_pair, bias):
    low = lax.broadcasted_iota(jnp.int32, query_pair.shape, 1) < HEAD
    zero = jnp.zeros_like(query_pair)
    one = jnp.ones_like(value_pair)
    queries = (jnp.where(low, query_pair, zero), jnp.where(low, zero, query_pair))
    values = (jnp.where(low, value_pair, one), jnp.where(low, one, value_pair))
    mixed = []
    for query_one, value_one in zip(queries, values):
        scores = lax.dot_general(
            query_one, key_pair, (((1,), (1,)), ((), ())), preferred_element_type=F32
        )
        masked = scores + bias
        exp_terms = jnp.exp(masked - jnp.max(masked, axis=1, keepdims=True)).astype(BF16)
        mixed.append(jnp.dot(exp_terms, value_one, preferred_element_type=F32))
    sums = jnp.where(low, mixed[0], mixed[1])
    totals = pltpu.roll(jnp.where(low, mixed[1], mixed[0]), HEAD, 1)
    return (sums / totals).astype(BF16)


def class_and_turn(place, per_class):
    kind = jnp.zeros_like(place)
    for bound in range(1, PAIR_CLASSES):
        kind = kind + jnp.where(place >= bound * per_class, 1, 0)
    return kind, place - per_class * kind


def fused_kernel(
    layers, tensors,
    q_hbm, k_hbm, v_hbm, ids_hbm, w_ref, res_hbm, out_ref,
    q_ref, k_ref, v_ref, ids_ref, res_ref,
    bias, acc, count_own, counts, w_full, attended, spilled, rows_all,
    core_out, core_in, mine, across_out, across_in, kept, summed, final_out, final_in,
    count_send, count_recv, w_send, w_recv, spill_send, spill_recv,
    own_send, relay_send, rows_recv, core_send, core_recv, across_send, across_recv,
    final_send, final_recv, load_sem, ids_sem, w_sem, res_sem,
):
    devices = layers * HALVES
    cap = q_ref.shape[0]
    width = q_ref.shape[1]
    half_rows = rows_all.shape[2]
    part_width = width // PARTS
    quarter = final_in.shape[2]
    per_class = half_rows // PAIR_CLASSES
    both = HALVES * half_rows
    p = lax.axis_index("pairs")
    t = lax.axis_index("tensor")
    z = p // HALVES
    y = p % HALVES
    x = t // 2
    core = t % 2
    beside = (z * HALVES + 1 - y, t)
    other_core = (p, x * 2 + 1 - core)
    other_chip = (p, (1 - x) * 2 + core)

    barrier = pltpu.get_barrier_semaphore()
    everyone = devices * tensors

    def greet(step, carry):
        number = lax.rem(p * tensors + t + step, everyone)
        pl.semaphore_signal(
            barrier, inc=1, device_id=(number // tensors, number % tensors), device_id_type=MESH
        )
        return carry

    loads = {}
    ids_load = pltpu.make_async_copy(ids_hbm, ids_ref, ids_sem)
    ids_load.start()
    for part in range(PARTS):
        columns = slice(part * part_width, (part + 1) * part_width)
        for which, (src, dst) in enumerate(((q_hbm, q_ref), (k_hbm, k_ref), (v_hbm, v_ref))):
            loads[part, which] = pltpu.make_async_copy(
                src.at[:, columns], dst.at[:, columns], load_sem.at[part, which]
            )
            loads[part, which].start()
    w_load = pltpu.make_async_copy(w_ref, w_full.at[y], w_sem)
    w_load.start()
    res_load = pltpu.make_async_copy(res_hbm, res_ref, res_sem)
    res_load.start()

    lax.fori_loop(1, everyone, greet, 0)
    ids_load.wait()

    ids_row = ids_ref[...].astype(F32)
    live = jnp.sum(jnp.where(ids_row < SLOTS, 1.0, 0.0), axis=1, keepdims=True)
    own_count = jnp.broadcast_to(live, count_own.shape).astype(jnp.int32)
    count_own[...] = own_count
    counts[p] = own_count
    ids_wide = jnp.broadcast_to(ids_row, (cap, cap))
    bias[...] = jnp.where(ids_wide == ids_wide.T, 0.0, -1e30)
    pl.semaphore_wait(barrier, everyone - 1)

    def remote(src, dst, sent, got, where_to):
        return pltpu.make_async_remote_copy(
            src_ref=src, dst_ref=dst, send_sem=sent, recv_sem=got,
            device_id=where_to, device_id_type=MESH,
        )

    pending = []
    for step in range(1, devices):
        peer = lax.rem(p + step, devices)
        copy = remote(count_own, counts.at[p], count_send.at[step], count_recv.at[p], (peer, t))
        copy.start()
        pending.append(copy)

    piece_rows = w_ref.shape[0] // WEIGHT_PIECES

    def weight_copy(piece, slot):
        rows = pl.ds(piece * piece_rows, piece_rows)
        return remote(
            w_ref.at[rows], w_full.at[slot, rows], w_send.at[piece], w_recv.at[piece], beside
        )

    def send_weights(first, last):
        for piece in range(first, last):
            copy = weight_copy(piece, y)
            copy.start()
            pending.append(copy)

    def rows_copy(block, part, sent, layer):
        here = rows_all.at[block, part]
        return remote(here, here, sent, rows_recv.at[block, part], (layer * HALVES + y, t))

    spill_from = pl.multiple_of((1 - y) * (cap - SPILL), 16)

    def spill_copy(part):
        return remote(
            attended.at[pl.ds(spill_from, SPILL), pl.ds(part * part_width, part_width)], spilled.at[part],
            spill_send.at[part], spill_recv.at[part], beside,
        )

    def attend_part(part):
        for which in range(3):
            loads[part, which].wait()
        for pair in range(part_width // (2 * HEAD)):
            lanes = slice(part * part_width + pair * 2 * HEAD, part * part_width + (pair + 1) * 2 * HEAD)
            attended[:, lanes] = attend_pair(
                q_ref[:, lanes], k_ref[:, lanes], v_ref[:, lanes], bias[...]
            )
        copy = spill_copy(part)
        copy.start()
        pending.append(copy)

    send_weights(0, 1)
    attend_part(0)
    attend_part(1)
    send_weights(1, 2)

    for step in range(1, devices):
        source = lax.rem(p + step, devices)
        remote(count_own, counts.at[source], count_send.at[0], count_recv.at[source], (source, t)).wait_recv()

    def start_of(block):
        total = jnp.zeros((1, cap), jnp.int32)
        for earlier in range(devices):
            total = total + jnp.where(earlier < block, counts[earlier, 0:1, :], 0)
        return total

    live_first = counts[HALVES * z, 0:1, :]
    live_second = counts[HALVES * z + 1, 0:1, :]
    second_at = both - live_second - ((both - live_first - live_second) & 7)
    start_pair = start_of(HALVES * z)
    kind, turn = class_and_turn(lax.broadcasted_iota(jnp.int32, (half_rows, cap), 0), per_class)
    slot = y * half_rows + ((kind - start_pair) & 7) + 8 * turn
    column = lax.broadcasted_iota(jnp.int32, (half_rows, cap), 1)
    row_first = slot
    row_second = slot - second_at
    row_own = jnp.where(y == 0, row_first, row_second)
    row_peer = jnp.where(y == 0, row_second, row_first)
    live_own = jnp.where(y == 0, live_first, live_second)
    live_peer = jnp.where(y == 0, live_second, live_first)
    pick_own = jnp.where((column == row_own) & (column < live_own), 1.0, 0.0).astype(BF16)
    peer_from = y * (cap - SPILL)
    pick_peer = jnp.where((column == row_peer - peer_from) & (column + peer_from < live_peer), 1.0, 0.0)
    pick_peer = pick_peer.astype(BF16)[:, :SPILL]

    def share_part(part):
        spill_copy(part).wait_recv()
        columns = slice(part * part_width, (part + 1) * part_width)
        packed = jnp.dot(pick_own, attended[:, columns], preferred_element_type=F32)
        packed = packed + jnp.dot(pick_peer, spilled[part], preferred_element_type=F32)
        rows_all[z, part] = packed.astype(BF16)

        @pl.when(z < layers - 1)
        def _():
            rows_copy(z, part, own_send.at[0, part], z + 1).start()

        @pl.when(z > 0)
        def _():
            rows_copy(z, part, own_send.at[1, part], z - 1).start()

    share_part(0)
    for part in range(2, PARTS):
        attend_part(part)
        if part < PARTS - 1:
            send_weights(part, part + 1)
        else:
            send_weights(part, WEIGHT_PIECES)
        share_part(part - 1)
    share_part(PARTS - 1)

    order = (
        z,
        jnp.where(z % 2 == 0, z + 1, z - 1),
        jnp.where(z < 2, 2, 1),
        jnp.where(z < 2, 3, 0),
    )
    inner = (z > 0) & (z < layers - 1)

    def take_rows(turn_index, relay):
        block = order[turn_index]
        onward = jnp.where(block < z, z + 1, z - 1)
        for part in range(PARTS):
            copy = rows_copy(block, part, relay_send.at[turn_index, part], onward)
            copy.wait_recv()
            if relay:
                copy.start()

    def take_inner(turn_index):
        @pl.when(inner)
        def _():
            take_rows(turn_index, True)

    def take_outer(turn_index):
        @pl.when(jnp.logical_not(inner))
        def _():
            take_rows(turn_index, False)

    def partial_of(turn_index, side, first=0, end=width):
        rows = jnp.concatenate(
            [
                rows_all[order[turn_index], part]
                for part in range(first // part_width, end // part_width)
            ],
            axis=1,
        )
        return jnp.dot(rows, w_full[side, first:end, :], preferred_element_type=F32)

    def core_copy(turn_index):
        return remote(
            core_out.at[turn_index], core_in.at[turn_index],
            core_send.at[turn_index], core_recv.at[turn_index], other_core,
        )

    def across_copy(turn_index):
        return remote(
            across_out.at[turn_index], across_in.at[turn_index],
            across_send.at[turn_index], across_recv.at[turn_index], other_chip,
        )

    def multiply(turn_index, side):
        hand_out(turn_index, side, partial_of(turn_index, side))

    def hand_out(turn_index, side, total):
        value = total.astype(BF16)

        @pl.when(core == side)
        def _():
            mine[turn_index] = value

        @pl.when(core != side)
        def _():
            core_out[turn_index] = value
            core_copy(turn_index).start()

    def add_cores(turn_index):
        core_copy(turn_index).wait_recv()
        total = mine[turn_index].astype(F32) + core_in[turn_index].astype(F32)
        left, right = total[:, :quarter], total[:, quarter:]
        across_out[turn_index] = jnp.where(x == 0, right, left).astype(BF16)
        kept[turn_index] = jnp.where(x == 0, left, right)
        across_copy(turn_index).start()

    def add_chips(turn_index):
        across_copy(turn_index).wait_recv()
        total = kept[turn_index] + across_in[turn_index].astype(F32)
        summed[:, order[turn_index]] = total.reshape(PAIR_CLASSES, per_class, quarter)

    last = layers - 1
    w_load.wait()
    multiply(0, y)
    for turn_index in range(1, last):
        take_inner(turn_index)
        take_outer(turn_index)
        multiply(turn_index, y)

        @pl.when(core == y)
        def _():
            add_cores(turn_index - 1)

    take_inner(last)

    @pl.when(core == y)
    def _():
        add_cores(last - 1)

    half_pieces = WEIGHT_PIECES // 2
    half_depth = width // 2
    for piece in range(half_pieces):
        weight_copy(piece, 1 - y).wait_recv()
    for turn_index in range(last):
        acc[turn_index] = partial_of(turn_index, 1 - y, 0, half_depth)
    for piece in range(half_pieces, WEIGHT_PIECES):
        weight_copy(piece, 1 - y).wait_recv()

    for turn_index in range(last):
        hand_out(
            turn_index, 1 - y,
            acc[turn_index] + partial_of(turn_index, 1 - y, half_depth, width),
        )

        @pl.when(core != y)
        def _():
            add_cores(turn_index)

    take_outer(last)
    core_out[last] = partial_of(last, 1 - core).astype(BF16)
    core_copy(last).start()
    mine[last] = partial_of(last, core).astype(BF16)
    add_cores(last)
    for turn_index in range(layers):
        add_chips(turn_index)

    final_out[...] = summed[...].reshape(final_out.shape).astype(BF16)
    source_slot = y * tensors + core * 2 + x
    to_self = z == t

    def final_copy(step):
        peer = lax.rem(p + step, devices)
        return remote(
            final_out.at[peer], final_in.at[source_slot],
            final_send.at[step], final_recv.at[source_slot], (peer, z),
        )

    for step in range(1, devices):
        copy = final_copy(step)
        copy.start()
        pending.append(copy)

    @pl.when(to_self)
    def _():
        final_in[source_slot] = final_out[p]

    @pl.when(jnp.logical_not(to_self))
    def _():
        final_copy(0).start()

    place_shape = (half_rows, HALVES * layers * per_class)
    lane = lax.broadcasted_iota(jnp.int32, (1, place_shape[1]), 1)
    side = jnp.where(lane >= layers * per_class, 1, 0)
    lane = lane - side * layers * per_class
    layer = jnp.zeros_like(lane)
    for bound in range(1, layers):
        layer = layer + jnp.where(lane >= bound * per_class, 1, 0)
    lane = lane - layer * per_class
    spot = jnp.zeros_like(lane) - 1
    count_width = place_shape[1]
    for block in range(layers):
        first = counts[HALVES * block, 0:1, :][:, :count_width]
        second = counts[HALVES * block + 1, 0:1, :][:, :count_width]
        begin = start_of(HALVES * block)[:, :count_width]
        second_from = both - second - ((both - first - second) & 7)
        where_at = side * half_rows + ((p - begin) & 7) + 8 * lane
        number = jnp.where(
            where_at < first, begin + where_at,
            jnp.where(
                (where_at >= second_from) & (where_at < second_from + second),
                begin + first + where_at - second_from, -8,
            ),
        )
        spot = jnp.where(layer == block, number >> 3, spot)
    place = jnp.where(
        lax.broadcasted_iota(jnp.int32, place_shape, 0) == spot, 1.0, 0.0
    ).astype(BF16)

    for half in range(HALVES):
        for piece in range(tensors):
            slot_index = half * tensors + piece
            from_self = (z == t) & (source_slot == slot_index)

            @pl.when(jnp.logical_not(from_self))
            def _():
                remote(
                    final_out.at[0], final_in.at[slot_index], final_send.at[0],
                    final_recv.at[slot_index], (lax.rem(p + 1, devices), t),
                ).wait_recv()

    res_load.wait()
    depth = layers * per_class
    for piece in range(tensors):
        columns = slice(piece * quarter, (piece + 1) * quarter)
        moved = res_ref[:, columns].astype(F32)
        for half in range(HALVES):
            moved = moved + jnp.dot(
                place[:, half * depth:(half + 1) * depth],
                final_in[half * tensors + piece], preferred_element_type=F32,
            )
        out_ref[:, columns] = moved.astype(BF16)

    for copy in pending:
        copy.wait_send()
    for turn_index in range(layers):
        core_copy(turn_index).wait_send()
        across_copy(turn_index).wait_send()
    for part in range(PARTS):
        @pl.when(z < layers - 1)
        def _():
            rows_copy(z, part, own_send.at[0, part], z + 1).wait_send()

        @pl.when(z > 0)
        def _():
            rows_copy(z, part, own_send.at[1, part], z - 1).wait_send()

    @pl.when(inner)
    def _():
        for turn_index in range(1, layers):
            block = order[turn_index]
            onward = jnp.where(block < z, z + 1, z - 1)
            for part in range(PARTS):
                rows_copy(block, part, relay_send.at[turn_index, part], onward).wait_send()

    @pl.when(jnp.logical_not(to_self))
    def _():
        final_copy(0).wait_send()


def fused_shards(layers, tensors, queries, key_rows, value_rows, pair_ids, out_weight, residual):
    devices = layers * HALVES
    cap, width = queries.shape
    half_rows = residual.shape[0]
    columns = out_weight.shape[1]
    quarter = columns // 2
    part_width = width // PARTS
    per_class = half_rows // PAIR_CLASSES
    depth = layers * per_class
    dma = pltpu.SemaphoreType.DMA
    vmem = pltpu.VMEM
    scratch = [
        vmem((cap, width), BF16), vmem((cap, width), BF16), vmem((cap, width), BF16),
        vmem((1, cap), jnp.int32),
        vmem(residual.shape, BF16),
        vmem((cap, cap), F32),
        vmem((layers - 1, half_rows, columns), F32),
        vmem((8, cap), jnp.int32),
        vmem((devices, 8, cap), jnp.int32),
        vmem((HALVES, width, columns), BF16),
        vmem((cap, width), BF16),
        vmem((PARTS, SPILL, part_width), BF16),
        vmem((layers, PARTS, half_rows, part_width), BF16),
        vmem((layers, half_rows, columns), BF16),
        vmem((layers, half_rows, columns), BF16),
        vmem((layers, half_rows, columns), BF16),
        vmem((layers, half_rows, quarter), BF16),
        vmem((layers, half_rows, quarter), BF16),
        vmem((layers, half_rows, quarter), F32),
        vmem((PAIR_CLASSES, layers, per_class, quarter), F32),
        vmem((devices, depth, quarter), BF16),
        vmem((HALVES * tensors, depth, quarter), BF16),
        dma((devices,)), dma((devices,)),
        dma((WEIGHT_PIECES,)), dma((WEIGHT_PIECES,)),
        dma((PARTS,)), dma((PARTS,)),
        dma((2, PARTS)), dma((layers, PARTS)), dma((layers, PARTS)),
        dma((layers,)), dma((layers,)),
        dma((layers,)), dma((layers,)),
        dma((devices,)), dma((HALVES * tensors,)),
        dma((PARTS, 3)), dma, dma, dma,
    ]
    in_vmem = pl.BlockSpec(memory_space=pltpu.VMEM)
    return pl.pallas_call(
        functools.partial(fused_kernel, layers, tensors),
        out_shape=jax.ShapeDtypeStruct(residual.shape, residual.dtype),
        in_specs=[pl.BlockSpec(memory_space=pl.ANY)] * 6,
        out_specs=in_vmem,
        scratch_shapes=scratch,
        compiler_params=pltpu.CompilerParams(
            collective_id=0, has_side_effects=True, vmem_limit_bytes=56 * 1024 * 1024
        ),
    )(queries, key_rows, value_rows, pair_ids.reshape(1, cap), out_weight, residual)


def fits_fused(mesh):
    layers = mesh.shape["pairs"] // HALVES
    return mesh.shape["tensor"] == 4 and layers == 4


def solution(mesh):
    in_specs = (
        P("pairs", "tensor"),
        P("pairs", "tensor"),
        P("pairs", "tensor"),
        P("pairs"),
        P("tensor", "pairs"),
        P("pairs", "tensor"),
    )
    out_specs = P("pairs", "tensor")
    per_device = shards
    if fits_fused(mesh):
        per_device = functools.partial(fused_shards, mesh.shape["pairs"] // HALVES, mesh.shape["tensor"])
    return jax.shard_map(per_device, mesh=mesh, in_specs=in_specs, out_specs=out_specs, check_vma=False)
```

```python
import functools

import jax
import jax.numpy as jnp
from jax import lax
from jax.experimental import pallas as pl
from jax.experimental.pallas import tpu as pltpu
from jax.sharding import PartitionSpec as P

HEAD = 64
SLOTS = 8


def carried_in(part, axis, combine, identity):
    place = lax.axis_index(axis)
    gathered = lax.all_gather(part, axis)
    state = jnp.zeros_like(part) + jnp.asarray(identity, part.dtype)

    def one(step, state):
        return combine(state, lax.dynamic_index_in_dim(gathered, step, 0, False))

    return lax.fori_loop(0, place, one, state)


def attend_group(query_part, key_part, value_part, allowed):
    scores = jnp.einsum("qhd,khd->hqk", query_part, key_part, preferred_element_type=jnp.float32)
    masked = jnp.where(allowed[None], scores, -1e30)
    row_top = jnp.max(masked, axis=2, keepdims=True)
    exp_terms = jnp.where(allowed[None], jnp.exp(masked - row_top), 0.0)
    row_total = jnp.maximum(jnp.sum(exp_terms, axis=2, keepdims=True), 1.0)
    weights = (exp_terms / row_total).astype(jnp.bfloat16)
    mixed = jnp.einsum("hqk,khd->qhd", weights, value_part, preferred_element_type=jnp.float32)
    return mixed.astype(jnp.bfloat16)


def add_counts(earlier, later):
    return earlier + later


def shards(queries, key_rows, value_rows, pair_ids, out_weight, residual):
    cap_rows = queries.shape[0]
    local_width = queries.shape[1]
    heads_local = local_width // HEAD
    group_size = 4
    balanced_rows = residual.shape[0]
    allowed = (pair_ids[:, None] == pair_ids[None, :]) & (pair_ids[:, None] < SLOTS)

    def split_heads(stacked):
        return stacked.reshape(cap_rows, heads_local // group_size, group_size, HEAD).transpose(
            1, 0, 2, 3
        )

    def per_group(operands):
        return attend_group(operands[0], operands[1], operands[2], allowed)

    grouped = lax.map(
        per_group, (split_heads(queries), split_heads(key_rows), split_heads(value_rows))
    )
    attended = grouped.transpose(1, 0, 2, 3).reshape(cap_rows, local_width)
    live_rows = jnp.sum((pair_ids < SLOTS).astype(jnp.int32))
    devices = lax.axis_size("pairs")
    row_start = carried_in(live_rows.reshape(1), "pairs", add_counts, jnp.zeros((1,), jnp.int32))[0]
    partial_value = jnp.dot(
        attended,
        lax.all_gather(out_weight, "pairs", axis=1, tiled=True),
        preferred_element_type=jnp.float32,
    )
    payload = lax.psum_scatter(
        partial_value.astype(jnp.bfloat16), "tensor", scatter_dimension=1, tiled=True
    )
    per_peer = cap_rows // devices
    feature_width = payload.shape[1]
    peer_index = jnp.arange(devices, dtype=jnp.int32)
    turn_index = jnp.arange(per_peer, dtype=jnp.int32)
    source_rows = ((peer_index - row_start) % devices)[:, None] + devices * turn_index[None, :]
    slot_index = jnp.where(
        source_rows < live_rows, (row_start + source_rows) // devices, balanced_rows
    ).astype(jnp.int32)
    outgoing = jnp.take(payload, source_rows.reshape(-1), axis=0).reshape(
        devices, per_peer, feature_width
    )
    incoming = lax.all_to_all(outgoing, "pairs", split_axis=0, concat_axis=0, tiled=True)
    incoming_slots = lax.all_to_all(slot_index, "pairs", split_axis=0, concat_axis=0, tiled=True)
    landed = jnp.zeros((balanced_rows, feature_width), payload.dtype)
    moved_rows = landed.at[incoming_slots.reshape(-1)].set(
        incoming.reshape(-1, feature_width), mode="drop"
    )
    return (residual.astype(jnp.float32) + moved_rows.astype(jnp.float32)).astype(jnp.bfloat16)


HALVES = 2
PARTS = 4
WEIGHT_PIECES = 8
SPILL = 80
BATCHES = 2
PAIR_CLASSES = 8
MESH = pl.DeviceIdType.MESH
BF16 = jnp.bfloat16
F32 = jnp.float32


def attend_pair(query_pair, key_pair, value_pair, bias):
    low = lax.broadcasted_iota(jnp.int32, query_pair.shape, 1) < HEAD
    zero = jnp.zeros_like(query_pair)
    one = jnp.ones_like(value_pair)
    queries = (jnp.where(low, query_pair, zero), jnp.where(low, zero, query_pair))
    values = (jnp.where(low, value_pair, one), jnp.where(low, one, value_pair))
    mixed = []
    for query_one, value_one in zip(queries, values):
        scores = lax.dot_general(
            query_one, key_pair, (((1,), (1,)), ((), ())), preferred_element_type=F32
        )
        masked = scores + bias
        exp_terms = jnp.exp(masked - jnp.max(masked, axis=1, keepdims=True)).astype(BF16)
        mixed.append(jnp.dot(exp_terms, value_one, preferred_element_type=F32))
    sums = jnp.where(low, mixed[0], mixed[1])
    totals = pltpu.roll(jnp.where(low, mixed[1], mixed[0]), HEAD, 1)
    return (sums / totals).astype(BF16)


def class_and_turn(place, per_class):
    kind = jnp.zeros_like(place)
    for bound in range(1, PAIR_CLASSES):
        kind = kind + jnp.where(place >= bound * per_class, 1, 0)
    return kind, place - per_class * kind


def fused_kernel(
    layers, tensors,
    q_hbm, k_hbm, v_hbm, ids_hbm, w_ref, res_hbm, out_ref,
    q_ref, k_ref, v_ref, ids_ref, res_ref,
    bias, acc, count_own, counts, w_full, attended, spilled, rows_all,
    core_out, core_in, mine, across_out, across_in, kept, summed, final_out, final_in,
    count_send, count_recv, w_send, w_recv, spill_send, spill_recv,
    own_send, relay_send, rows_recv, core_send, core_recv, across_send, across_recv,
    final_send, final_recv, load_sem, ids_sem, w_sem, res_sem,
):
    devices = layers * HALVES
    cap = q_ref.shape[0]
    width = q_ref.shape[1]
    half_rows = rows_all.shape[2]
    part_width = width // PARTS
    quarter = kept.shape[2]
    per_class = half_rows // PAIR_CLASSES
    both = HALVES * half_rows
    p = lax.axis_index("pairs")
    t = lax.axis_index("tensor")
    z = p // HALVES
    y = p % HALVES
    x = t // 2
    core = t % 2
    beside = (z * HALVES + 1 - y, t)
    other_core = (p, x * 2 + 1 - core)
    other_chip = (p, (1 - x) * 2 + core)

    barrier = pltpu.get_barrier_semaphore()
    everyone = devices * tensors

    def greet(step, carry):
        number = lax.rem(p * tensors + t + step, everyone)
        pl.semaphore_signal(
            barrier, inc=1, device_id=(number // tensors, number % tensors), device_id_type=MESH
        )
        return carry

    loads = {}
    ids_load = pltpu.make_async_copy(ids_hbm, ids_ref, ids_sem)
    ids_load.start()
    for part in range(PARTS):
        columns = slice(part * part_width, (part + 1) * part_width)
        for which, (src, dst) in enumerate(((q_hbm, q_ref), (k_hbm, k_ref), (v_hbm, v_ref))):
            loads[part, which] = pltpu.make_async_copy(
                src.at[:, columns], dst.at[:, columns], load_sem.at[part, which]
            )
            loads[part, which].start()
    w_load = pltpu.make_async_copy(w_ref, w_full.at[y], w_sem)
    w_load.start()
    res_load = pltpu.make_async_copy(res_hbm, res_ref, res_sem)
    res_load.start()

    lax.fori_loop(1, everyone, greet, 0)
    ids_load.wait()

    ids_row = ids_ref[...].astype(F32)
    live = jnp.sum(jnp.where(ids_row < SLOTS, 1.0, 0.0), axis=1, keepdims=True)
    own_count = jnp.broadcast_to(live, count_own.shape).astype(jnp.int32)
    count_own[...] = own_count
    counts[p] = own_count
    ids_wide = jnp.broadcast_to(ids_row, (cap, cap))
    bias[...] = jnp.where(ids_wide == ids_wide.T, 0.0, -1e30)
    pl.semaphore_wait(barrier, everyone - 1)

    def remote(src, dst, sent, got, where_to):
        return pltpu.make_async_remote_copy(
            src_ref=src, dst_ref=dst, send_sem=sent, recv_sem=got,
            device_id=where_to, device_id_type=MESH,
        )

    pending = []
    for step in range(1, devices):
        peer = lax.rem(p + step, devices)
        copy = remote(count_own, counts.at[p], count_send.at[step], count_recv.at[p], (peer, t))
        copy.start()
        pending.append(copy)

    piece_rows = w_ref.shape[0] // WEIGHT_PIECES

    def weight_copy(piece, slot):
        rows = pl.ds(piece * piece_rows, piece_rows)
        return remote(
            w_ref.at[rows], w_full.at[slot, rows], w_send.at[piece], w_recv.at[piece], beside
        )

    def send_weights(first, last):
        for piece in range(first, last):
            copy = weight_copy(piece, y)
            copy.start()
            pending.append(copy)

    def rows_copy(block, part, sent, layer):
        here = rows_all.at[block, part]
        return remote(here, here, sent, rows_recv.at[block, part], (layer * HALVES + y, t))

    spill_from = pl.multiple_of((1 - y) * (cap - SPILL), 16)

    def spill_copy(part):
        return remote(
            attended.at[pl.ds(spill_from, SPILL), pl.ds(part * part_width, part_width)], spilled.at[part],
            spill_send.at[part], spill_recv.at[part], beside,
        )

    def attend_part(part):
        for which in range(3):
            loads[part, which].wait()
        for pair in range(part_width // (2 * HEAD)):
            lanes = slice(part * part_width + pair * 2 * HEAD, part * part_width + (pair + 1) * 2 * HEAD)
            attended[:, lanes] = attend_pair(
                q_ref[:, lanes], k_ref[:, lanes], v_ref[:, lanes], bias[...]
            )
        copy = spill_copy(part)
        copy.start()
        pending.append(copy)

    send_weights(0, 1)
    attend_part(0)
    attend_part(1)
    send_weights(1, 2)

    for step in range(1, devices):
        source = lax.rem(p + step, devices)
        remote(count_own, counts.at[source], count_send.at[0], count_recv.at[source], (source, t)).wait_recv()

    def start_of(block):
        total = jnp.zeros((1, cap), jnp.int32)
        for earlier in range(devices):
            total = total + jnp.where(earlier < block, counts[earlier, 0:1, :], 0)
        return total

    live_first = counts[HALVES * z, 0:1, :]
    live_second = counts[HALVES * z + 1, 0:1, :]
    second_at = both - live_second - ((both - live_first - live_second) & 7)
    start_pair = start_of(HALVES * z)
    kind, turn = class_and_turn(lax.broadcasted_iota(jnp.int32, (half_rows, cap), 0), per_class)
    slot = y * half_rows + ((kind - start_pair) & 7) + 8 * turn
    column = lax.broadcasted_iota(jnp.int32, (half_rows, cap), 1)
    row_first = slot
    row_second = slot - second_at
    row_own = jnp.where(y == 0, row_first, row_second)
    row_peer = jnp.where(y == 0, row_second, row_first)
    live_own = jnp.where(y == 0, live_first, live_second)
    live_peer = jnp.where(y == 0, live_second, live_first)
    pick_own = jnp.where((column == row_own) & (column < live_own), 1.0, 0.0).astype(BF16)
    peer_from = y * (cap - SPILL)
    pick_peer = jnp.where((column == row_peer - peer_from) & (column + peer_from < live_peer), 1.0, 0.0)
    pick_peer = pick_peer.astype(BF16)[:, :SPILL]

    def share_part(part):
        spill_copy(part).wait_recv()
        columns = slice(part * part_width, (part + 1) * part_width)
        packed = jnp.dot(pick_own, attended[:, columns], preferred_element_type=F32)
        packed = packed + jnp.dot(pick_peer, spilled[part], preferred_element_type=F32)
        rows_all[z, part] = packed.astype(BF16)

        @pl.when(z < layers - 1)
        def _():
            rows_copy(z, part, own_send.at[0, part], z + 1).start()

        @pl.when(z > 0)
        def _():
            rows_copy(z, part, own_send.at[1, part], z - 1).start()

    share_part(0)
    for part in range(2, PARTS):
        attend_part(part)
        if part < PARTS - 1:
            send_weights(part, part + 1)
        else:
            send_weights(part, WEIGHT_PIECES)
        share_part(part - 1)
    share_part(PARTS - 1)

    def order_of(layer):
        return (
            layer,
            jnp.where(layer % 2 == 0, layer + 1, layer - 1),
            jnp.where(layer < 2, 2, 1),
            jnp.where(layer < 2, 3, 0),
        )

    order = order_of(z)
    inner = (z > 0) & (z < layers - 1)

    def take_rows(turn_index, relay):
        block = order[turn_index]
        onward = jnp.where(block < z, z + 1, z - 1)
        for part in range(PARTS):
            copy = rows_copy(block, part, relay_send.at[turn_index, part], onward)
            copy.wait_recv()
            if relay:
                copy.start()

    def take_inner(turn_index):
        @pl.when(inner)
        def _():
            take_rows(turn_index, True)

    def take_outer(turn_index):
        @pl.when(jnp.logical_not(inner))
        def _():
            take_rows(turn_index, False)

    def partial_of(turn_index, side, first=0, end=width):
        rows = jnp.concatenate(
            [
                rows_all[order[turn_index], part]
                for part in range(first // part_width, end // part_width)
            ],
            axis=1,
        )
        return jnp.dot(rows, w_full[side, first:end, :], preferred_element_type=F32)

    def core_copy(turn_index):
        return remote(
            core_out.at[turn_index], core_in.at[turn_index],
            core_send.at[turn_index], core_recv.at[turn_index], other_core,
        )

    def across_copy(turn_index):
        return remote(
            across_out.at[turn_index], across_in.at[turn_index],
            across_send.at[turn_index], across_recv.at[turn_index], other_chip,
        )

    def multiply(turn_index, side):
        hand_out(turn_index, side, partial_of(turn_index, side))

    def hand_out(turn_index, side, total):
        value = total.astype(BF16)

        @pl.when(core == side)
        def _():
            mine[turn_index] = value

        @pl.when(core != side)
        def _():
            core_out[turn_index] = value
            core_copy(turn_index).start()

    def add_cores(turn_index):
        core_copy(turn_index).wait_recv()
        total = mine[turn_index].astype(F32) + core_in[turn_index].astype(F32)
        left, right = total[:, :quarter], total[:, quarter:]
        across_out[turn_index] = jnp.where(x == 0, right, left).astype(BF16)
        kept[turn_index] = jnp.where(x == 0, left, right)
        across_copy(turn_index).start()

    def add_chips(turn_index):
        across_copy(turn_index).wait_recv()
        total = kept[turn_index] + across_in[turn_index].astype(F32)
        summed[:, turn_index] = total.reshape(PAIR_CLASSES, per_class, quarter)

    batch_turns = layers // BATCHES
    batch_rows = batch_turns * per_class
    source_slot = y * tensors + core * 2 + x
    to_self = z == t

    def final_copy(batch, step):
        peer = lax.rem(p + step, devices)
        return remote(
            final_out.at[batch, peer], final_in.at[batch, source_slot],
            final_send.at[batch, step], final_recv.at[batch, source_slot], (peer, z),
        )

    def spread(batch):
        turns = slice(batch * batch_turns, (batch + 1) * batch_turns)
        for turn_index in range(layers)[turns]:
            add_chips(turn_index)
        final_out[batch] = summed[:, turns].reshape(devices, batch_rows, quarter).astype(BF16)
        for step in range(1, devices):
            final_copy(batch, step).start()

        @pl.when(to_self)
        def _():
            final_in[batch, source_slot] = final_out[batch, p]

        @pl.when(jnp.logical_not(to_self))
        def _():
            final_copy(batch, 0).start()

    last = layers - 1
    w_load.wait()
    multiply(0, y)
    for turn_index in range(1, last):
        take_inner(turn_index)
        take_outer(turn_index)
        multiply(turn_index, y)

        @pl.when(core == y)
        def _():
            add_cores(turn_index - 1)

    take_inner(last)

    @pl.when(core == y)
    def _():
        add_cores(last - 1)
        spread(0)

    half_pieces = WEIGHT_PIECES // 2
    half_depth = width // 2
    for piece in range(half_pieces):
        weight_copy(piece, 1 - y).wait_recv()
    for turn_index in range(last):
        acc[turn_index] = partial_of(turn_index, 1 - y, 0, half_depth)
    for piece in range(half_pieces, WEIGHT_PIECES):
        weight_copy(piece, 1 - y).wait_recv()

    for turn_index in range(last):
        hand_out(
            turn_index, 1 - y,
            acc[turn_index] + partial_of(turn_index, 1 - y, half_depth, width),
        )

        @pl.when(core != y)
        def _():
            add_cores(turn_index)

    @pl.when(core != y)
    def _():
        spread(0)

    take_outer(last)
    core_out[last] = partial_of(last, 1 - core).astype(BF16)
    core_copy(last).start()
    mine[last] = partial_of(last, core).astype(BF16)
    add_cores(last)
    for batch in range(1, BATCHES):
        spread(batch)

    place_shape = (half_rows, HALVES * layers * per_class)
    lane = lax.broadcasted_iota(jnp.int32, (1, place_shape[1]), 1)
    side = jnp.where(lane >= layers * per_class, 1, 0)
    lane = lane - side * layers * per_class
    layer = jnp.zeros_like(lane)
    for bound in range(1, layers):
        layer = layer + jnp.where(lane >= bound * per_class, 1, 0)
    lane = lane - layer * per_class
    spot = jnp.zeros_like(lane) - 1
    count_width = place_shape[1]
    sender_order = order_of(t)
    for turn_index in range(layers):
        block = sender_order[turn_index]
        first = counts[HALVES * block, 0:1, :][:, :count_width]
        second = counts[HALVES * block + 1, 0:1, :][:, :count_width]
        begin = start_of(HALVES * block)[:, :count_width]
        second_from = both - second - ((both - first - second) & 7)
        where_at = side * half_rows + ((p - begin) & 7) + 8 * lane
        number = jnp.where(
            where_at < first, begin + where_at,
            jnp.where(
                (where_at >= second_from) & (where_at < second_from + second),
                begin + first + where_at - second_from, -8,
            ),
        )
        spot = jnp.where(layer == turn_index, number >> 3, spot)
    place = jnp.where(
        lax.broadcasted_iota(jnp.int32, place_shape, 0) == spot, 1.0, 0.0
    ).astype(BF16)

    for batch in range(BATCHES):
        for slot_index in range(HALVES * tensors):
            @pl.when(jnp.logical_not(to_self & (source_slot == slot_index)))
            def _():
                remote(
                    final_out.at[batch, 0], final_in.at[batch, slot_index], final_send.at[batch, 0],
                    final_recv.at[batch, slot_index], (lax.rem(p + 1, devices), t),
                ).wait_recv()

    res_load.wait()
    for piece in range(tensors):
        columns = slice(piece * quarter, (piece + 1) * quarter)
        rows = jnp.concatenate(
            [
                final_in[batch, half * tensors + piece]
                for half in range(HALVES) for batch in range(BATCHES)
            ],
            axis=0,
        )
        moved = jnp.dot(place, rows, preferred_element_type=F32)
        out_ref[:, columns] = (res_ref[:, columns].astype(F32) + moved).astype(BF16)

    for copy in pending:
        copy.wait_send()
    for turn_index in range(layers):
        core_copy(turn_index).wait_send()
        across_copy(turn_index).wait_send()
    for part in range(PARTS):
        @pl.when(z < layers - 1)
        def _():
            rows_copy(z, part, own_send.at[0, part], z + 1).wait_send()

        @pl.when(z > 0)
        def _():
            rows_copy(z, part, own_send.at[1, part], z - 1).wait_send()

    @pl.when(inner)
    def _():
        for turn_index in range(1, layers):
            block = order[turn_index]
            onward = jnp.where(block < z, z + 1, z - 1)
            for part in range(PARTS):
                rows_copy(block, part, relay_send.at[turn_index, part], onward).wait_send()

    for batch in range(BATCHES):
        for step in range(1, devices):
            final_copy(batch, step).wait_send()

        @pl.when(jnp.logical_not(to_self))
        def _():
            final_copy(batch, 0).wait_send()


def fused_shards(layers, tensors, queries, key_rows, value_rows, pair_ids, out_weight, residual):
    devices = layers * HALVES
    cap, width = queries.shape
    half_rows = residual.shape[0]
    columns = out_weight.shape[1]
    quarter = columns // 2
    part_width = width // PARTS
    per_class = half_rows // PAIR_CLASSES
    batch_rows = layers // BATCHES * per_class
    dma = pltpu.SemaphoreType.DMA
    vmem = pltpu.VMEM
    scratch = [
        vmem((cap, width), BF16), vmem((cap, width), BF16), vmem((cap, width), BF16),
        vmem((1, cap), jnp.int32),
        vmem(residual.shape, BF16),
        vmem((cap, cap), F32),
        vmem((layers - 1, half_rows, columns), F32),
        vmem((8, cap), jnp.int32),
        vmem((devices, 8, cap), jnp.int32),
        vmem((HALVES, width, columns), BF16),
        vmem((cap, width), BF16),
        vmem((PARTS, SPILL, part_width), BF16),
        vmem((layers, PARTS, half_rows, part_width), BF16),
        vmem((layers, half_rows, columns), BF16),
        vmem((layers, half_rows, columns), BF16),
        vmem((layers, half_rows, columns), BF16),
        vmem((layers, half_rows, quarter), BF16),
        vmem((layers, half_rows, quarter), BF16),
        vmem((layers, half_rows, quarter), F32),
        vmem((PAIR_CLASSES, layers, per_class, quarter), F32),
        vmem((BATCHES, devices, batch_rows, quarter), BF16),
        vmem((BATCHES, HALVES * tensors, batch_rows, quarter), BF16),
        dma((devices,)), dma((devices,)),
        dma((WEIGHT_PIECES,)), dma((WEIGHT_PIECES,)),
        dma((PARTS,)), dma((PARTS,)),
        dma((2, PARTS)), dma((layers, PARTS)), dma((layers, PARTS)),
        dma((layers,)), dma((layers,)),
        dma((layers,)), dma((layers,)),
        dma((BATCHES, devices)), dma((BATCHES, HALVES * tensors)),
        dma((PARTS, 3)), dma, dma, dma,
    ]
    in_vmem = pl.BlockSpec(memory_space=pltpu.VMEM)
    return pl.pallas_call(
        functools.partial(fused_kernel, layers, tensors),
        out_shape=jax.ShapeDtypeStruct(residual.shape, residual.dtype),
        in_specs=[pl.BlockSpec(memory_space=pl.ANY)] * 6,
        out_specs=in_vmem,
        scratch_shapes=scratch,
        compiler_params=pltpu.CompilerParams(
            collective_id=0, has_side_effects=True, vmem_limit_bytes=56 * 1024 * 1024
        ),
    )(queries, key_rows, value_rows, pair_ids.reshape(1, cap), out_weight, residual)


def fits_fused(mesh):
    layers = mesh.shape["pairs"] // HALVES
    return mesh.shape["tensor"] == 4 and layers == 4


def solution(mesh):
    in_specs = (
        P("pairs", "tensor"),
        P("pairs", "tensor"),
        P("pairs", "tensor"),
        P("pairs"),
        P("tensor", "pairs"),
        P("pairs", "tensor"),
    )
    out_specs = P("pairs", "tensor")
    per_device = shards
    if fits_fused(mesh):
        per_device = functools.partial(fused_shards, mesh.shape["pairs"] // HALVES, mesh.shape["tensor"])
    return jax.shard_map(per_device, mesh=mesh, in_specs=in_specs, out_specs=out_specs, check_vma=False)
```

```python
import functools

import jax
import jax.numpy as jnp
from jax import lax
from jax.experimental import pallas as pl
from jax.experimental.pallas import tpu as pltpu
from jax.sharding import PartitionSpec as P

HEAD = 64
SLOTS = 8


def carried_in(part, axis, combine, identity):
    place = lax.axis_index(axis)
    gathered = lax.all_gather(part, axis)
    state = jnp.zeros_like(part) + jnp.asarray(identity, part.dtype)

    def one(step, state):
        return combine(state, lax.dynamic_index_in_dim(gathered, step, 0, False))

    return lax.fori_loop(0, place, one, state)


def attend_group(query_part, key_part, value_part, allowed):
    scores = jnp.einsum("qhd,khd->hqk", query_part, key_part, preferred_element_type=jnp.float32)
    masked = jnp.where(allowed[None], scores, -1e30)
    row_top = jnp.max(masked, axis=2, keepdims=True)
    exp_terms = jnp.where(allowed[None], jnp.exp(masked - row_top), 0.0)
    row_total = jnp.maximum(jnp.sum(exp_terms, axis=2, keepdims=True), 1.0)
    weights = (exp_terms / row_total).astype(jnp.bfloat16)
    mixed = jnp.einsum("hqk,khd->qhd", weights, value_part, preferred_element_type=jnp.float32)
    return mixed.astype(jnp.bfloat16)


def add_counts(earlier, later):
    return earlier + later


def shards(queries, key_rows, value_rows, pair_ids, out_weight, residual):
    cap_rows = queries.shape[0]
    local_width = queries.shape[1]
    heads_local = local_width // HEAD
    group_size = 4
    balanced_rows = residual.shape[0]
    allowed = (pair_ids[:, None] == pair_ids[None, :]) & (pair_ids[:, None] < SLOTS)

    def split_heads(stacked):
        return stacked.reshape(cap_rows, heads_local // group_size, group_size, HEAD).transpose(
            1, 0, 2, 3
        )

    def per_group(operands):
        return attend_group(operands[0], operands[1], operands[2], allowed)

    grouped = lax.map(
        per_group, (split_heads(queries), split_heads(key_rows), split_heads(value_rows))
    )
    attended = grouped.transpose(1, 0, 2, 3).reshape(cap_rows, local_width)
    live_rows = jnp.sum((pair_ids < SLOTS).astype(jnp.int32))
    devices = lax.axis_size("pairs")
    row_start = carried_in(live_rows.reshape(1), "pairs", add_counts, jnp.zeros((1,), jnp.int32))[0]
    partial_value = jnp.dot(
        attended,
        lax.all_gather(out_weight, "pairs", axis=1, tiled=True),
        preferred_element_type=jnp.float32,
    )
    payload = lax.psum_scatter(
        partial_value.astype(jnp.bfloat16), "tensor", scatter_dimension=1, tiled=True
    )
    per_peer = cap_rows // devices
    feature_width = payload.shape[1]
    peer_index = jnp.arange(devices, dtype=jnp.int32)
    turn_index = jnp.arange(per_peer, dtype=jnp.int32)
    source_rows = ((peer_index - row_start) % devices)[:, None] + devices * turn_index[None, :]
    slot_index = jnp.where(
        source_rows < live_rows, (row_start + source_rows) // devices, balanced_rows
    ).astype(jnp.int32)
    outgoing = jnp.take(payload, source_rows.reshape(-1), axis=0).reshape(
        devices, per_peer, feature_width
    )
    incoming = lax.all_to_all(outgoing, "pairs", split_axis=0, concat_axis=0, tiled=True)
    incoming_slots = lax.all_to_all(slot_index, "pairs", split_axis=0, concat_axis=0, tiled=True)
    landed = jnp.zeros((balanced_rows, feature_width), payload.dtype)
    moved_rows = landed.at[incoming_slots.reshape(-1)].set(
        incoming.reshape(-1, feature_width), mode="drop"
    )
    return (residual.astype(jnp.float32) + moved_rows.astype(jnp.float32)).astype(jnp.bfloat16)


HALVES = 2
PARTS = 4
WEIGHT_PIECES = 8
SPILL = 80
BATCHES = 2
PAIR_CLASSES = 8
MESH = pl.DeviceIdType.MESH
BF16 = jnp.bfloat16
F32 = jnp.float32


def attend_pair(query_pair, key_pair, value_pair, bias):
    low = lax.broadcasted_iota(jnp.int32, query_pair.shape, 1) < HEAD
    zero = jnp.zeros_like(query_pair)
    one = jnp.ones_like(value_pair)
    queries = (jnp.where(low, query_pair, zero), jnp.where(low, zero, query_pair))
    values = (jnp.where(low, value_pair, one), jnp.where(low, one, value_pair))
    mixed = []
    for query_one, value_one in zip(queries, values):
        scores = lax.dot_general(
            query_one, key_pair, (((1,), (1,)), ((), ())), preferred_element_type=F32
        )
        masked = scores + bias
        exp_terms = jnp.exp(masked - jnp.max(masked, axis=1, keepdims=True)).astype(BF16)
        mixed.append(jnp.dot(exp_terms, value_one, preferred_element_type=F32))
    sums = jnp.where(low, mixed[0], mixed[1])
    totals = pltpu.roll(jnp.where(low, mixed[1], mixed[0]), HEAD, 1)
    return (sums / totals).astype(BF16)


def class_and_turn(place, per_class):
    kind = jnp.zeros_like(place)
    for bound in range(1, PAIR_CLASSES):
        kind = kind + jnp.where(place >= bound * per_class, 1, 0)
    return kind, place - per_class * kind


def fused_kernel(
    layers, tensors,
    q_hbm, k_hbm, v_hbm, ids_hbm, w_ref, res_hbm, out_ref,
    q_ref, k_ref, v_ref, ids_ref, res_ref,
    bias, acc, count_own, counts, w_full, attended, spilled, rows_all,
    core_out, core_in, mine, across_out, across_in, kept, summed, final_out, final_in,
    count_send, count_recv, w_send, w_recv, spill_send, spill_recv,
    own_send, relay_send, rows_recv, core_send, core_recv, across_send, across_recv,
    final_send, final_recv, load_sem, ids_sem, w_sem, res_sem,
):
    devices = layers * HALVES
    cap = q_ref.shape[0]
    width = q_ref.shape[1]
    half_rows = rows_all.shape[2]
    part_width = width // PARTS
    quarter = kept.shape[2]
    per_class = half_rows // PAIR_CLASSES
    both = HALVES * half_rows
    p = lax.axis_index("pairs")
    t = lax.axis_index("tensor")
    z = p // HALVES
    y = p % HALVES
    x = t // 2
    core = t % 2
    beside = (z * HALVES + 1 - y, t)
    other_core = (p, x * 2 + 1 - core)
    other_chip = (p, (1 - x) * 2 + core)

    barrier = pltpu.get_barrier_semaphore()
    everyone = devices * tensors

    def greet(step, carry):
        number = lax.rem(p * tensors + t + step, everyone)
        pl.semaphore_signal(
            barrier, inc=1, device_id=(number // tensors, number % tensors), device_id_type=MESH
        )
        return carry

    loads = {}
    ids_load = pltpu.make_async_copy(ids_hbm, ids_ref, ids_sem)
    ids_load.start()
    for part in range(PARTS):
        columns = slice(part * part_width, (part + 1) * part_width)
        for which, (src, dst) in enumerate(((q_hbm, q_ref), (k_hbm, k_ref), (v_hbm, v_ref))):
            loads[part, which] = pltpu.make_async_copy(
                src.at[:, columns], dst.at[:, columns], load_sem.at[part, which]
            )
            loads[part, which].start()
    w_load = pltpu.make_async_copy(w_ref, w_full.at[y], w_sem)
    w_load.start()
    res_load = pltpu.make_async_copy(res_hbm, res_ref, res_sem)
    res_load.start()

    lax.fori_loop(1, everyone, greet, 0)
    ids_load.wait()

    ids_row = ids_ref[...].astype(F32)
    live = jnp.sum(jnp.where(ids_row < SLOTS, 1.0, 0.0), axis=1, keepdims=True)
    own_count = jnp.broadcast_to(live, count_own.shape).astype(jnp.int32)
    count_own[...] = own_count
    counts[p] = own_count
    ids_wide = jnp.broadcast_to(ids_row, (cap, cap))
    bias[...] = jnp.where(ids_wide == ids_wide.T, 0.0, -1e30)
    pl.semaphore_wait(barrier, everyone - 1)

    def remote(src, dst, sent, got, where_to):
        return pltpu.make_async_remote_copy(
            src_ref=src, dst_ref=dst, send_sem=sent, recv_sem=got,
            device_id=where_to, device_id_type=MESH,
        )

    pending = []
    for step in range(1, devices):
        peer = lax.rem(p + step, devices)
        copy = remote(count_own, counts.at[p], count_send.at[step], count_recv.at[p], (peer, t))
        copy.start()
        pending.append(copy)

    piece_rows = w_ref.shape[0] // WEIGHT_PIECES

    def weight_copy(piece, slot):
        rows = pl.ds(piece * piece_rows, piece_rows)
        return remote(
            w_ref.at[rows], w_full.at[slot, rows], w_send.at[piece], w_recv.at[piece], beside
        )

    def send_weights(first, last):
        for piece in range(first, last):
            copy = weight_copy(piece, y)
            copy.start()
            pending.append(copy)

    def rows_copy(block, part, sent, layer):
        here = rows_all.at[block, part]
        return remote(here, here, sent, rows_recv.at[block, part], (layer * HALVES + y, t))

    spill_from = pl.multiple_of((1 - y) * (cap - SPILL), 16)

    def spill_copy(part):
        return remote(
            attended.at[pl.ds(spill_from, SPILL), pl.ds(part * part_width, part_width)], spilled.at[part],
            spill_send.at[part], spill_recv.at[part], beside,
        )

    def attend_part(part):
        for which in range(3):
            loads[part, which].wait()
        for pair in range(part_width // (2 * HEAD)):
            lanes = slice(part * part_width + pair * 2 * HEAD, part * part_width + (pair + 1) * 2 * HEAD)
            attended[:, lanes] = attend_pair(
                q_ref[:, lanes], k_ref[:, lanes], v_ref[:, lanes], bias[...]
            )
        copy = spill_copy(part)
        copy.start()
        pending.append(copy)

    send_weights(0, 1)
    attend_part(0)
    attend_part(1)
    send_weights(1, 2)

    for step in range(1, devices):
        source = lax.rem(p + step, devices)
        remote(count_own, counts.at[source], count_send.at[0], count_recv.at[source], (source, t)).wait_recv()

    def start_of(block):
        total = jnp.zeros((1, cap), jnp.int32)
        for earlier in range(devices):
            total = total + jnp.where(earlier < block, counts[earlier, 0:1, :], 0)
        return total

    live_first = counts[HALVES * z, 0:1, :]
    live_second = counts[HALVES * z + 1, 0:1, :]
    second_at = both - live_second - ((both - live_first - live_second) & 7)
    start_pair = start_of(HALVES * z)
    kind, turn = class_and_turn(lax.broadcasted_iota(jnp.int32, (half_rows, cap), 0), per_class)
    slot = y * half_rows + ((kind - start_pair) & 7) + 8 * turn
    column = lax.broadcasted_iota(jnp.int32, (half_rows, cap), 1)
    row_first = slot
    row_second = slot - second_at
    row_own = jnp.where(y == 0, row_first, row_second)
    row_peer = jnp.where(y == 0, row_second, row_first)
    live_own = jnp.where(y == 0, live_first, live_second)
    live_peer = jnp.where(y == 0, live_second, live_first)
    pick_own = jnp.where((column == row_own) & (column < live_own), 1.0, 0.0).astype(BF16)
    peer_from = y * (cap - SPILL)
    pick_peer = jnp.where((column == row_peer - peer_from) & (column + peer_from < live_peer), 1.0, 0.0)
    pick_peer = pick_peer.astype(BF16)[:, :SPILL]

    def share_part(part):
        spill_copy(part).wait_recv()
        columns = slice(part * part_width, (part + 1) * part_width)
        packed = jnp.dot(pick_own, attended[:, columns], preferred_element_type=F32)
        packed = packed + jnp.dot(pick_peer, spilled[part], preferred_element_type=F32)
        rows_all[z, part] = packed.astype(BF16)

        @pl.when(z < layers - 1)
        def _():
            rows_copy(z, part, own_send.at[0, part], z + 1).start()

        @pl.when(z > 0)
        def _():
            rows_copy(z, part, own_send.at[1, part], z - 1).start()

    share_part(0)
    for part in range(2, PARTS):
        attend_part(part)
        if part < PARTS - 1:
            send_weights(part, part + 1)
        else:
            send_weights(part, WEIGHT_PIECES)
        share_part(part - 1)
    share_part(PARTS - 1)

    def order_of(layer):
        return (
            layer,
            jnp.where(layer % 2 == 0, layer + 1, layer - 1),
            jnp.where(layer < 2, 2, 1),
            jnp.where(layer < 2, 3, 0),
        )

    order = order_of(z)
    inner = (z > 0) & (z < layers - 1)

    def take_row(turn_index, part, relay):
        block = order[turn_index]
        onward = jnp.where(block < z, z + 1, z - 1)
        copy = rows_copy(block, part, relay_send.at[turn_index, part], onward)
        copy.wait_recv()
        if relay:
            copy.start()

    def take_outer(turn_index):
        @pl.when(jnp.logical_not(inner))
        def _():
            for part in range(PARTS):
                take_row(turn_index, part, False)

    def partial_of(turn_index, side, first=0, end=width):
        rows = jnp.concatenate(
            [
                rows_all[order[turn_index], part]
                for part in range(first // part_width, end // part_width)
            ],
            axis=1,
        )
        return jnp.dot(rows, w_full[side, first:end, :], preferred_element_type=F32)

    def core_copy(turn_index):
        return remote(
            core_out.at[turn_index], core_in.at[turn_index],
            core_send.at[turn_index], core_recv.at[turn_index], other_core,
        )

    def across_copy(turn_index):
        return remote(
            across_out.at[turn_index], across_in.at[turn_index],
            across_send.at[turn_index], across_recv.at[turn_index], other_chip,
        )

    def multiply(turn_index, side):
        hand_out(turn_index, side, partial_of(turn_index, side))

    def hand_out(turn_index, side, total):
        value = total.astype(BF16)

        @pl.when(core == side)
        def _():
            mine[turn_index] = value

        @pl.when(core != side)
        def _():
            core_out[turn_index] = value
            core_copy(turn_index).start()

    def add_cores(turn_index):
        core_copy(turn_index).wait_recv()
        total = mine[turn_index].astype(F32) + core_in[turn_index].astype(F32)
        left, right = total[:, :quarter], total[:, quarter:]
        across_out[turn_index] = jnp.where(x == 0, right, left).astype(BF16)
        kept[turn_index] = jnp.where(x == 0, left, right)
        across_copy(turn_index).start()

    def add_chips(turn_index):
        across_copy(turn_index).wait_recv()
        total = kept[turn_index] + across_in[turn_index].astype(F32)
        summed[:, turn_index] = total.reshape(PAIR_CLASSES, per_class, quarter)

    batch_turns = layers // BATCHES
    batch_rows = batch_turns * per_class
    source_slot = y * tensors + core * 2 + x
    to_self = z == t

    def final_copy(batch, step):
        peer = lax.rem(p + step, devices)
        return remote(
            final_out.at[batch, peer], final_in.at[batch, source_slot],
            final_send.at[batch, step], final_recv.at[batch, source_slot], (peer, z),
        )

    def spread(batch):
        turns = slice(batch * batch_turns, (batch + 1) * batch_turns)
        for turn_index in range(layers)[turns]:
            add_chips(turn_index)
        final_out[batch] = summed[:, turns].reshape(devices, batch_rows, quarter).astype(BF16)
        for step in range(1, devices):
            final_copy(batch, step).start()

        @pl.when(to_self)
        def _():
            final_in[batch, source_slot] = final_out[batch, p]

        @pl.when(jnp.logical_not(to_self))
        def _():
            final_copy(batch, 0).start()

    last = layers - 1
    @pl.when(inner)
    def _():
        for part in range(PARTS):
            for turn_index in range(1, last):
                take_row(turn_index, part, True)
        for part in range(PARTS):
            take_row(last, part, True)

    w_load.wait()
    multiply(0, y)
    for turn_index in range(1, last):
        take_outer(turn_index)
        multiply(turn_index, y)

        @pl.when(core == y)
        def _():
            add_cores(turn_index - 1)

    @pl.when(core == y)
    def _():
        add_cores(last - 1)
        spread(0)

    half_pieces = WEIGHT_PIECES // 2
    half_depth = width // 2
    for piece in range(half_pieces):
        weight_copy(piece, 1 - y).wait_recv()
    for turn_index in range(last):
        acc[turn_index] = partial_of(turn_index, 1 - y, 0, half_depth)
    for piece in range(half_pieces, WEIGHT_PIECES):
        weight_copy(piece, 1 - y).wait_recv()

    for turn_index in range(last):
        hand_out(
            turn_index, 1 - y,
            acc[turn_index] + partial_of(turn_index, 1 - y, half_depth, width),
        )

        @pl.when(core != y)
        def _():
            add_cores(turn_index)

    @pl.when(core != y)
    def _():
        spread(0)

    take_outer(last)
    core_out[last] = partial_of(last, 1 - core).astype(BF16)
    core_copy(last).start()
    mine[last] = partial_of(last, core).astype(BF16)
    add_cores(last)
    for batch in range(1, BATCHES):
        spread(batch)

    place_shape = (half_rows, HALVES * layers * per_class)
    lane = lax.broadcasted_iota(jnp.int32, (1, place_shape[1]), 1)
    side = jnp.where(lane >= layers * per_class, 1, 0)
    lane = lane - side * layers * per_class
    layer = jnp.zeros_like(lane)
    for bound in range(1, layers):
        layer = layer + jnp.where(lane >= bound * per_class, 1, 0)
    lane = lane - layer * per_class
    spot = jnp.zeros_like(lane) - 1
    count_width = place_shape[1]
    sender_order = order_of(t)
    for turn_index in range(layers):
        block = sender_order[turn_index]
        first = counts[HALVES * block, 0:1, :][:, :count_width]
        second = counts[HALVES * block + 1, 0:1, :][:, :count_width]
        begin = start_of(HALVES * block)[:, :count_width]
        second_from = both - second - ((both - first - second) & 7)
        where_at = side * half_rows + ((p - begin) & 7) + 8 * lane
        number = jnp.where(
            where_at < first, begin + where_at,
            jnp.where(
                (where_at >= second_from) & (where_at < second_from + second),
                begin + first + where_at - second_from, -8,
            ),
        )
        spot = jnp.where(layer == turn_index, number >> 3, spot)
    place = jnp.where(
        lax.broadcasted_iota(jnp.int32, place_shape, 0) == spot, 1.0, 0.0
    ).astype(BF16)

    for batch in range(BATCHES):
        for slot_index in range(HALVES * tensors):
            @pl.when(jnp.logical_not(to_self & (source_slot == slot_index)))
            def _():
                remote(
                    final_out.at[batch, 0], final_in.at[batch, slot_index], final_send.at[batch, 0],
                    final_recv.at[batch, slot_index], (lax.rem(p + 1, devices), t),
                ).wait_recv()

    res_load.wait()
    for piece in range(tensors):
        columns = slice(piece * quarter, (piece + 1) * quarter)
        rows = jnp.concatenate(
            [
                final_in[batch, half * tensors + piece]
                for half in range(HALVES) for batch in range(BATCHES)
            ],
            axis=0,
        )
        moved = jnp.dot(place, rows, preferred_element_type=F32)
        out_ref[:, columns] = (res_ref[:, columns].astype(F32) + moved).astype(BF16)

    for copy in pending:
        copy.wait_send()
    for turn_index in range(layers):
        core_copy(turn_index).wait_send()
        across_copy(turn_index).wait_send()
    for part in range(PARTS):
        @pl.when(z < layers - 1)
        def _():
            rows_copy(z, part, own_send.at[0, part], z + 1).wait_send()

        @pl.when(z > 0)
        def _():
            rows_copy(z, part, own_send.at[1, part], z - 1).wait_send()

    @pl.when(inner)
    def _():
        for turn_index in range(1, layers):
            block = order[turn_index]
            onward = jnp.where(block < z, z + 1, z - 1)
            for part in range(PARTS):
                rows_copy(block, part, relay_send.at[turn_index, part], onward).wait_send()

    for batch in range(BATCHES):
        for step in range(1, devices):
            final_copy(batch, step).wait_send()

        @pl.when(jnp.logical_not(to_self))
        def _():
            final_copy(batch, 0).wait_send()


def fused_shards(layers, tensors, queries, key_rows, value_rows, pair_ids, out_weight, residual):
    devices = layers * HALVES
    cap, width = queries.shape
    half_rows = residual.shape[0]
    columns = out_weight.shape[1]
    quarter = columns // 2
    part_width = width // PARTS
    per_class = half_rows // PAIR_CLASSES
    batch_rows = layers // BATCHES * per_class
    dma = pltpu.SemaphoreType.DMA
    vmem = pltpu.VMEM
    scratch = [
        vmem((cap, width), BF16), vmem((cap, width), BF16), vmem((cap, width), BF16),
        vmem((1, cap), jnp.int32),
        vmem(residual.shape, BF16),
        vmem((cap, cap), F32),
        vmem((layers - 1, half_rows, columns), F32),
        vmem((8, cap), jnp.int32),
        vmem((devices, 8, cap), jnp.int32),
        vmem((HALVES, width, columns), BF16),
        vmem((cap, width), BF16),
        vmem((PARTS, SPILL, part_width), BF16),
        vmem((layers, PARTS, half_rows, part_width), BF16),
        vmem((layers, half_rows, columns), BF16),
        vmem((layers, half_rows, columns), BF16),
        vmem((layers, half_rows, columns), BF16),
        vmem((layers, half_rows, quarter), BF16),
        vmem((layers, half_rows, quarter), BF16),
        vmem((layers, half_rows, quarter), F32),
        vmem((PAIR_CLASSES, layers, per_class, quarter), F32),
        vmem((BATCHES, devices, batch_rows, quarter), BF16),
        vmem((BATCHES, HALVES * tensors, batch_rows, quarter), BF16),
        dma((devices,)), dma((devices,)),
        dma((WEIGHT_PIECES,)), dma((WEIGHT_PIECES,)),
        dma((PARTS,)), dma((PARTS,)),
        dma((2, PARTS)), dma((layers, PARTS)), dma((layers, PARTS)),
        dma((layers,)), dma((layers,)),
        dma((layers,)), dma((layers,)),
        dma((BATCHES, devices)), dma((BATCHES, HALVES * tensors)),
        dma((PARTS, 3)), dma, dma, dma,
    ]
    in_vmem = pl.BlockSpec(memory_space=pltpu.VMEM)
    return pl.pallas_call(
        functools.partial(fused_kernel, layers, tensors),
        out_shape=jax.ShapeDtypeStruct(residual.shape, residual.dtype),
        in_specs=[pl.BlockSpec(memory_space=pl.ANY)] * 6,
        out_specs=in_vmem,
        scratch_shapes=scratch,
        compiler_params=pltpu.CompilerParams(
            collective_id=0, has_side_effects=True, vmem_limit_bytes=56 * 1024 * 1024
        ),
    )(queries, key_rows, value_rows, pair_ids.reshape(1, cap), out_weight, residual)


def fits_fused(mesh):
    layers = mesh.shape["pairs"] // HALVES
    return mesh.shape["tensor"] == 4 and layers == 4


def solution(mesh):
    in_specs = (
        P("pairs", "tensor"),
        P("pairs", "tensor"),
        P("pairs", "tensor"),
        P("pairs"),
        P("tensor", "pairs"),
        P("pairs", "tensor"),
    )
    out_specs = P("pairs", "tensor")
    per_device = shards
    if fits_fused(mesh):
        per_device = functools.partial(fused_shards, mesh.shape["pairs"] // HALVES, mesh.shape["tensor"])
    return jax.shard_map(per_device, mesh=mesh, in_specs=in_specs, out_specs=out_specs, check_vma=False)
```

```python
import functools

import jax
import jax.numpy as jnp
from jax import lax
from jax.experimental import pallas as pl
from jax.experimental.pallas import tpu as pltpu
from jax.sharding import PartitionSpec as P

HEAD = 64
SLOTS = 8


def carried_in(part, axis, combine, identity):
    place = lax.axis_index(axis)
    gathered = lax.all_gather(part, axis)
    state = jnp.zeros_like(part) + jnp.asarray(identity, part.dtype)

    def one(step, state):
        return combine(state, lax.dynamic_index_in_dim(gathered, step, 0, False))

    return lax.fori_loop(0, place, one, state)


def attend_group(query_part, key_part, value_part, allowed):
    scores = jnp.einsum("qhd,khd->hqk", query_part, key_part, preferred_element_type=jnp.float32)
    masked = jnp.where(allowed[None], scores, -1e30)
    row_top = jnp.max(masked, axis=2, keepdims=True)
    exp_terms = jnp.where(allowed[None], jnp.exp(masked - row_top), 0.0)
    row_total = jnp.maximum(jnp.sum(exp_terms, axis=2, keepdims=True), 1.0)
    weights = (exp_terms / row_total).astype(jnp.bfloat16)
    mixed = jnp.einsum("hqk,khd->qhd", weights, value_part, preferred_element_type=jnp.float32)
    return mixed.astype(jnp.bfloat16)


def add_counts(earlier, later):
    return earlier + later


def shards(queries, key_rows, value_rows, pair_ids, out_weight, residual):
    cap_rows = queries.shape[0]
    local_width = queries.shape[1]
    heads_local = local_width // HEAD
    group_size = 4
    balanced_rows = residual.shape[0]
    allowed = (pair_ids[:, None] == pair_ids[None, :]) & (pair_ids[:, None] < SLOTS)

    def split_heads(stacked):
        return stacked.reshape(cap_rows, heads_local // group_size, group_size, HEAD).transpose(
            1, 0, 2, 3
        )

    def per_group(operands):
        return attend_group(operands[0], operands[1], operands[2], allowed)

    grouped = lax.map(
        per_group, (split_heads(queries), split_heads(key_rows), split_heads(value_rows))
    )
    attended = grouped.transpose(1, 0, 2, 3).reshape(cap_rows, local_width)
    live_rows = jnp.sum((pair_ids < SLOTS).astype(jnp.int32))
    devices = lax.axis_size("pairs")
    row_start = carried_in(live_rows.reshape(1), "pairs", add_counts, jnp.zeros((1,), jnp.int32))[0]
    partial_value = jnp.dot(
        attended,
        lax.all_gather(out_weight, "pairs", axis=1, tiled=True),
        preferred_element_type=jnp.float32,
    )
    payload = lax.psum_scatter(
        partial_value.astype(jnp.bfloat16), "tensor", scatter_dimension=1, tiled=True
    )
    per_peer = cap_rows // devices
    feature_width = payload.shape[1]
    peer_index = jnp.arange(devices, dtype=jnp.int32)
    turn_index = jnp.arange(per_peer, dtype=jnp.int32)
    source_rows = ((peer_index - row_start) % devices)[:, None] + devices * turn_index[None, :]
    slot_index = jnp.where(
        source_rows < live_rows, (row_start + source_rows) // devices, balanced_rows
    ).astype(jnp.int32)
    outgoing = jnp.take(payload, source_rows.reshape(-1), axis=0).reshape(
        devices, per_peer, feature_width
    )
    incoming = lax.all_to_all(outgoing, "pairs", split_axis=0, concat_axis=0, tiled=True)
    incoming_slots = lax.all_to_all(slot_index, "pairs", split_axis=0, concat_axis=0, tiled=True)
    landed = jnp.zeros((balanced_rows, feature_width), payload.dtype)
    moved_rows = landed.at[incoming_slots.reshape(-1)].set(
        incoming.reshape(-1, feature_width), mode="drop"
    )
    return (residual.astype(jnp.float32) + moved_rows.astype(jnp.float32)).astype(jnp.bfloat16)


HALVES = 2
PARTS = 4
WEIGHT_PIECES = 8
SPILL = 80
BATCHES = 2
PAIR_CLASSES = 8
MESH = pl.DeviceIdType.MESH
BF16 = jnp.bfloat16
F32 = jnp.float32


def attend_pair(query_pair, key_pair, value_pair, bias):
    low = lax.broadcasted_iota(jnp.int32, query_pair.shape, 1) < HEAD
    zero = jnp.zeros_like(query_pair)
    one = jnp.ones_like(value_pair)
    queries = (jnp.where(low, query_pair, zero), jnp.where(low, zero, query_pair))
    values = (jnp.where(low, value_pair, one), jnp.where(low, one, value_pair))
    mixed = []
    for query_one, value_one in zip(queries, values):
        scores = lax.dot_general(
            query_one, key_pair, (((1,), (1,)), ((), ())), preferred_element_type=F32
        )
        masked = scores + bias
        exp_terms = jnp.exp(masked - jnp.max(masked, axis=1, keepdims=True)).astype(BF16)
        mixed.append(jnp.dot(exp_terms, value_one, preferred_element_type=F32))
    sums = jnp.where(low, mixed[0], mixed[1])
    totals = pltpu.roll(jnp.where(low, mixed[1], mixed[0]), HEAD, 1)
    return (sums / totals).astype(BF16)


def class_and_turn(place, per_class):
    kind = jnp.zeros_like(place)
    for bound in range(1, PAIR_CLASSES):
        kind = kind + jnp.where(place >= bound * per_class, 1, 0)
    return kind, place - per_class * kind


def fused_kernel(
    layers, tensors,
    q_hbm, k_hbm, v_hbm, ids_hbm, w_ref, res_hbm, out_ref,
    q_ref, k_ref, v_ref, ids_ref, res_ref,
    bias, acc, count_own, counts, w_full, attended, spilled, rows_all,
    core_out, core_in, mine, across_out, across_in, kept, summed, final_out, final_in,
    count_send, count_recv, w_send, w_recv, spill_send, spill_recv,
    own_send, relay_send, rows_recv, core_send, core_recv, across_send, across_recv,
    final_send, final_recv, load_sem, ids_sem, w_sem, res_sem,
):
    devices = layers * HALVES
    cap = q_ref.shape[0]
    width = q_ref.shape[1]
    half_rows = rows_all.shape[2]
    part_width = width // PARTS
    quarter = kept.shape[2]
    per_class = half_rows // PAIR_CLASSES
    both = HALVES * half_rows
    p = lax.axis_index("pairs")
    t = lax.axis_index("tensor")
    z = p // HALVES
    y = p % HALVES
    x = t // 2
    core = t % 2
    beside = (z * HALVES + 1 - y, t)
    other_core = (p, x * 2 + 1 - core)
    other_chip = (p, (1 - x) * 2 + core)

    barrier = pltpu.get_barrier_semaphore()
    everyone = devices * tensors

    def greet(step, carry):
        number = lax.rem(p * tensors + t + step, everyone)
        pl.semaphore_signal(
            barrier, inc=1, device_id=(number // tensors, number % tensors), device_id_type=MESH
        )
        return carry

    loads = {}
    ids_load = pltpu.make_async_copy(ids_hbm, ids_ref, ids_sem)
    ids_load.start()
    for part in range(PARTS):
        columns = slice(part * part_width, (part + 1) * part_width)
        for which, (src, dst) in enumerate(((q_hbm, q_ref), (k_hbm, k_ref), (v_hbm, v_ref))):
            loads[part, which] = pltpu.make_async_copy(
                src.at[:, columns], dst.at[:, columns], load_sem.at[part, which]
            )
            loads[part, which].start()
    w_load = pltpu.make_async_copy(w_ref, w_full.at[y], w_sem)
    w_load.start()
    res_load = pltpu.make_async_copy(res_hbm, res_ref, res_sem)
    res_load.start()

    lax.fori_loop(1, everyone, greet, 0)
    ids_load.wait()

    ids_row = ids_ref[...].astype(F32)
    live = jnp.sum(jnp.where(ids_row < SLOTS, 1.0, 0.0), axis=1, keepdims=True)
    own_count = jnp.broadcast_to(live, count_own.shape).astype(jnp.int32)
    count_own[...] = own_count
    counts[p] = own_count
    ids_wide = jnp.broadcast_to(ids_row, (cap, cap))
    bias[...] = jnp.where(ids_wide == ids_wide.T, 0.0, -1e30)
    pl.semaphore_wait(barrier, everyone - 1)

    def remote(src, dst, sent, got, where_to):
        return pltpu.make_async_remote_copy(
            src_ref=src, dst_ref=dst, send_sem=sent, recv_sem=got,
            device_id=where_to, device_id_type=MESH,
        )

    pending = []
    for step in range(1, devices):
        peer = lax.rem(p + step, devices)
        copy = remote(count_own, counts.at[p], count_send.at[step], count_recv.at[p], (peer, t))
        copy.start()
        pending.append(copy)

    piece_rows = w_ref.shape[0] // WEIGHT_PIECES

    def weight_copy(piece, slot):
        rows = pl.ds(piece * piece_rows, piece_rows)
        return remote(
            w_ref.at[rows], w_full.at[slot, rows], w_send.at[piece], w_recv.at[piece], beside
        )

    def send_weights(first, last):
        for piece in range(first, last):
            copy = weight_copy(piece, y)
            copy.start()
            pending.append(copy)

    def rows_copy(block, part, sent, layer):
        here = rows_all.at[block, part]
        return remote(here, here, sent, rows_recv.at[block, part], (layer * HALVES + y, t))

    spill_from = pl.multiple_of((1 - y) * (cap - SPILL), 16)

    def spill_copy(part):
        return remote(
            attended.at[pl.ds(spill_from, SPILL), pl.ds(part * part_width, part_width)], spilled.at[part],
            spill_send.at[part], spill_recv.at[part], beside,
        )

    def attend_part(part):
        for which in range(3):
            loads[part, which].wait()
        for pair in range(part_width // (2 * HEAD)):
            lanes = slice(part * part_width + pair * 2 * HEAD, part * part_width + (pair + 1) * 2 * HEAD)
            attended[:, lanes] = attend_pair(
                q_ref[:, lanes], k_ref[:, lanes], v_ref[:, lanes], bias[...]
            )
        copy = spill_copy(part)
        copy.start()
        pending.append(copy)

    send_weights(0, 2)
    attend_part(0)
    attend_part(1)
    send_weights(2, 3)

    for step in range(1, devices):
        source = lax.rem(p + step, devices)
        remote(count_own, counts.at[source], count_send.at[0], count_recv.at[source], (source, t)).wait_recv()

    def start_of(block):
        total = jnp.zeros((1, cap), jnp.int32)
        for earlier in range(devices):
            total = total + jnp.where(earlier < block, counts[earlier, 0:1, :], 0)
        return total

    live_first = counts[HALVES * z, 0:1, :]
    live_second = counts[HALVES * z + 1, 0:1, :]
    second_at = both - live_second - ((both - live_first - live_second) & 7)
    start_pair = start_of(HALVES * z)
    kind, turn = class_and_turn(lax.broadcasted_iota(jnp.int32, (half_rows, cap), 0), per_class)
    slot = y * half_rows + ((kind - start_pair) & 7) + 8 * turn
    column = lax.broadcasted_iota(jnp.int32, (half_rows, cap), 1)
    row_first = slot
    row_second = slot - second_at
    row_own = jnp.where(y == 0, row_first, row_second)
    row_peer = jnp.where(y == 0, row_second, row_first)
    live_own = jnp.where(y == 0, live_first, live_second)
    live_peer = jnp.where(y == 0, live_second, live_first)
    pick_own = jnp.where((column == row_own) & (column < live_own), 1.0, 0.0).astype(BF16)
    peer_from = y * (cap - SPILL)
    pick_peer = jnp.where((column == row_peer - peer_from) & (column + peer_from < live_peer), 1.0, 0.0)
    pick_peer = pick_peer.astype(BF16)[:, :SPILL]

    def share_part(part):
        spill_copy(part).wait_recv()
        columns = slice(part * part_width, (part + 1) * part_width)
        packed = jnp.dot(pick_own, attended[:, columns], preferred_element_type=F32)
        packed = packed + jnp.dot(pick_peer, spilled[part], preferred_element_type=F32)
        rows_all[z, part] = packed.astype(BF16)

        @pl.when(z < layers - 1)
        def _():
            rows_copy(z, part, own_send.at[0, part], z + 1).start()

        @pl.when(z > 0)
        def _():
            rows_copy(z, part, own_send.at[1, part], z - 1).start()

    share_part(0)
    for part in range(2, PARTS):
        attend_part(part)
        if part < PARTS - 1:
            send_weights(part + 1, part + 2)
        else:
            send_weights(part + 1, WEIGHT_PIECES)
        share_part(part - 1)
    share_part(PARTS - 1)

    def order_of(layer):
        return (
            layer,
            jnp.where(layer % 2 == 0, layer + 1, layer - 1),
            jnp.where(layer < 2, 2, 1),
            jnp.where(layer < 2, 3, 0),
        )

    order = order_of(z)
    inner = (z > 0) & (z < layers - 1)

    def take_row(turn_index, part, relay):
        block = order[turn_index]
        onward = jnp.where(block < z, z + 1, z - 1)
        copy = rows_copy(block, part, relay_send.at[turn_index, part], onward)
        copy.wait_recv()
        if relay:
            copy.start()

    def take_outer(turn_index):
        @pl.when(jnp.logical_not(inner))
        def _():
            for part in range(PARTS):
                take_row(turn_index, part, False)

    def partial_of(turn_index, side, first=0, end=width):
        rows = jnp.concatenate(
            [
                rows_all[order[turn_index], part]
                for part in range(first // part_width, end // part_width)
            ],
            axis=1,
        )
        return jnp.dot(rows, w_full[side, first:end, :], preferred_element_type=F32)

    def core_copy(turn_index):
        return remote(
            core_out.at[turn_index], core_in.at[turn_index],
            core_send.at[turn_index], core_recv.at[turn_index], other_core,
        )

    def across_copy(turn_index):
        return remote(
            across_out.at[turn_index], across_in.at[turn_index],
            across_send.at[turn_index], across_recv.at[turn_index], other_chip,
        )

    def multiply(turn_index, side):
        hand_out(turn_index, side, partial_of(turn_index, side))

    def hand_out(turn_index, side, total):
        value = total.astype(BF16)

        @pl.when(core == side)
        def _():
            mine[turn_index] = value

        @pl.when(core != side)
        def _():
            core_out[turn_index] = value
            core_copy(turn_index).start()

    def add_cores(turn_index):
        core_copy(turn_index).wait_recv()
        total = mine[turn_index].astype(F32) + core_in[turn_index].astype(F32)
        left, right = total[:, :quarter], total[:, quarter:]
        across_out[turn_index] = jnp.where(x == 0, right, left).astype(BF16)
        kept[turn_index] = jnp.where(x == 0, left, right)
        across_copy(turn_index).start()

    def add_chips(turn_index):
        across_copy(turn_index).wait_recv()
        total = kept[turn_index] + across_in[turn_index].astype(F32)
        summed[:, turn_index] = total.reshape(PAIR_CLASSES, per_class, quarter)

    batch_turns = layers // BATCHES
    batch_rows = batch_turns * per_class
    source_slot = y * tensors + core * 2 + x
    to_self = z == t

    def final_copy(batch, step):
        peer = lax.rem(p + step, devices)
        return remote(
            final_out.at[batch, peer], final_in.at[batch, source_slot],
            final_send.at[batch, step], final_recv.at[batch, source_slot], (peer, z),
        )

    def spread(batch):
        turns = slice(batch * batch_turns, (batch + 1) * batch_turns)
        for turn_index in range(layers)[turns]:
            add_chips(turn_index)
        final_out[batch] = summed[:, turns].reshape(devices, batch_rows, quarter).astype(BF16)
        for step in range(1, devices):
            final_copy(batch, step).start()

        @pl.when(to_self)
        def _():
            final_in[batch, source_slot] = final_out[batch, p]

        @pl.when(jnp.logical_not(to_self))
        def _():
            final_copy(batch, 0).start()

    last = layers - 1
    @pl.when(inner)
    def _():
        for part in range(PARTS):
            for turn_index in range(1, last):
                take_row(turn_index, part, True)
        for part in range(PARTS):
            take_row(last, part, True)

    w_load.wait()
    multiply(0, y)
    for turn_index in range(1, last):
        take_outer(turn_index)
        multiply(turn_index, y)

        @pl.when(core == y)
        def _():
            add_cores(turn_index - 1)

    @pl.when(core == y)
    def _():
        add_cores(last - 1)
        spread(0)

    half_pieces = WEIGHT_PIECES // 2
    half_depth = width // 2
    for piece in range(half_pieces):
        weight_copy(piece, 1 - y).wait_recv()
    for turn_index in range(last):
        acc[turn_index] = partial_of(turn_index, 1 - y, 0, half_depth)
    for piece in range(half_pieces, WEIGHT_PIECES):
        weight_copy(piece, 1 - y).wait_recv()

    for turn_index in range(last):
        hand_out(
            turn_index, 1 - y,
            acc[turn_index] + partial_of(turn_index, 1 - y, half_depth, width),
        )

        @pl.when(core != y)
        def _():
            add_cores(turn_index)

    @pl.when(core != y)
    def _():
        spread(0)

    take_outer(last)
    core_out[last] = partial_of(last, 1 - core).astype(BF16)
    core_copy(last).start()
    mine[last] = partial_of(last, core).astype(BF16)
    add_cores(last)
    for batch in range(1, BATCHES):
        spread(batch)

    place_shape = (half_rows, HALVES * layers * per_class)
    lane = lax.broadcasted_iota(jnp.int32, (1, place_shape[1]), 1)
    side = jnp.where(lane >= layers * per_class, 1, 0)
    lane = lane - side * layers * per_class
    layer = jnp.zeros_like(lane)
    for bound in range(1, layers):
        layer = layer + jnp.where(lane >= bound * per_class, 1, 0)
    lane = lane - layer * per_class
    spot = jnp.zeros_like(lane) - 1
    count_width = place_shape[1]
    sender_order = order_of(t)
    for turn_index in range(layers):
        block = sender_order[turn_index]
        first = counts[HALVES * block, 0:1, :][:, :count_width]
        second = counts[HALVES * block + 1, 0:1, :][:, :count_width]
        begin = start_of(HALVES * block)[:, :count_width]
        second_from = both - second - ((both - first - second) & 7)
        where_at = side * half_rows + ((p - begin) & 7) + 8 * lane
        number = jnp.where(
            where_at < first, begin + where_at,
            jnp.where(
                (where_at >= second_from) & (where_at < second_from + second),
                begin + first + where_at - second_from, -8,
            ),
        )
        spot = jnp.where(layer == turn_index, number >> 3, spot)
    place = jnp.where(
        lax.broadcasted_iota(jnp.int32, place_shape, 0) == spot, 1.0, 0.0
    ).astype(BF16)

    for batch in range(BATCHES):
        for slot_index in range(HALVES * tensors):
            @pl.when(jnp.logical_not(to_self & (source_slot == slot_index)))
            def _():
                remote(
                    final_out.at[batch, 0], final_in.at[batch, slot_index], final_send.at[batch, 0],
                    final_recv.at[batch, slot_index], (lax.rem(p + 1, devices), t),
                ).wait_recv()

    res_load.wait()
    for piece in range(tensors):
        columns = slice(piece * quarter, (piece + 1) * quarter)
        rows = jnp.concatenate(
            [
                final_in[batch, half * tensors + piece]
                for half in range(HALVES) for batch in range(BATCHES)
            ],
            axis=0,
        )
        moved = jnp.dot(place, rows, preferred_element_type=F32)
        out_ref[:, columns] = (res_ref[:, columns].astype(F32) + moved).astype(BF16)

    for copy in pending:
        copy.wait_send()
    for turn_index in range(layers):
        core_copy(turn_index).wait_send()
        across_copy(turn_index).wait_send()
    for part in range(PARTS):
        @pl.when(z < layers - 1)
        def _():
            rows_copy(z, part, own_send.at[0, part], z + 1).wait_send()

        @pl.when(z > 0)
        def _():
            rows_copy(z, part, own_send.at[1, part], z - 1).wait_send()

    @pl.when(inner)
    def _():
        for turn_index in range(1, layers):
            block = order[turn_index]
            onward = jnp.where(block < z, z + 1, z - 1)
            for part in range(PARTS):
                rows_copy(block, part, relay_send.at[turn_index, part], onward).wait_send()

    for batch in range(BATCHES):
        for step in range(1, devices):
            final_copy(batch, step).wait_send()

        @pl.when(jnp.logical_not(to_self))
        def _():
            final_copy(batch, 0).wait_send()


def fused_shards(layers, tensors, queries, key_rows, value_rows, pair_ids, out_weight, residual):
    devices = layers * HALVES
    cap, width = queries.shape
    half_rows = residual.shape[0]
    columns = out_weight.shape[1]
    quarter = columns // 2
    part_width = width // PARTS
    per_class = half_rows // PAIR_CLASSES
    batch_rows = layers // BATCHES * per_class
    dma = pltpu.SemaphoreType.DMA
    vmem = pltpu.VMEM
    scratch = [
        vmem((cap, width), BF16), vmem((cap, width), BF16), vmem((cap, width), BF16),
        vmem((1, cap), jnp.int32),
        vmem(residual.shape, BF16),
        vmem((cap, cap), F32),
        vmem((layers - 1, half_rows, columns), F32),
        vmem((8, cap), jnp.int32),
        vmem((devices, 8, cap), jnp.int32),
        vmem((HALVES, width, columns), BF16),
        vmem((cap, width), BF16),
        vmem((PARTS, SPILL, part_width), BF16),
        vmem((layers, PARTS, half_rows, part_width), BF16),
        vmem((layers, half_rows, columns), BF16),
        vmem((layers, half_rows, columns), BF16),
        vmem((layers, half_rows, columns), BF16),
        vmem((layers, half_rows, quarter), BF16),
        vmem((layers, half_rows, quarter), BF16),
        vmem((layers, half_rows, quarter), F32),
        vmem((PAIR_CLASSES, layers, per_class, quarter), F32),
        vmem((BATCHES, devices, batch_rows, quarter), BF16),
        vmem((BATCHES, HALVES * tensors, batch_rows, quarter), BF16),
        dma((devices,)), dma((devices,)),
        dma((WEIGHT_PIECES,)), dma((WEIGHT_PIECES,)),
        dma((PARTS,)), dma((PARTS,)),
        dma((2, PARTS)), dma((layers, PARTS)), dma((layers, PARTS)),
        dma((layers,)), dma((layers,)),
        dma((layers,)), dma((layers,)),
        dma((BATCHES, devices)), dma((BATCHES, HALVES * tensors)),
        dma((PARTS, 3)), dma, dma, dma,
    ]
    in_vmem = pl.BlockSpec(memory_space=pltpu.VMEM)
    return pl.pallas_call(
        functools.partial(fused_kernel, layers, tensors),
        out_shape=jax.ShapeDtypeStruct(residual.shape, residual.dtype),
        in_specs=[pl.BlockSpec(memory_space=pl.ANY)] * 6,
        out_specs=in_vmem,
        scratch_shapes=scratch,
        compiler_params=pltpu.CompilerParams(
            collective_id=0, has_side_effects=True, vmem_limit_bytes=56 * 1024 * 1024
        ),
    )(queries, key_rows, value_rows, pair_ids.reshape(1, cap), out_weight, residual)


def fits_fused(mesh):
    layers = mesh.shape["pairs"] // HALVES
    return mesh.shape["tensor"] == 4 and layers == 4


def solution(mesh):
    in_specs = (
        P("pairs", "tensor"),
        P("pairs", "tensor"),
        P("pairs", "tensor"),
        P("pairs"),
        P("tensor", "pairs"),
        P("pairs", "tensor"),
    )
    out_specs = P("pairs", "tensor")
    per_device = shards
    if fits_fused(mesh):
        per_device = functools.partial(fused_shards, mesh.shape["pairs"] // HALVES, mesh.shape["tensor"])
    return jax.shard_map(per_device, mesh=mesh, in_specs=in_specs, out_specs=out_specs, check_vma=False)
```
